32 devices in a mesh: section: 4 (over y, x), dp: 8 (over z, core).
Axes of the slice: x: 2, y: 2, z: 4, core: 2. Of those that a mesh axis runs over, the one named last changes fastest.
Arguments:
- patches: bfloat16 [2, 8, 256, 768], P(None, 'dp'), may hold values from -6 to 6
- lengths: int32 [2, 8], P(None, 'dp'), may hold values from 51 to 256, as said below
- qkv_weight: bfloat16 [4, 768, 2304], P('section'), may hold values from -0.21875 to 0.21875
- out_weight: bfloat16 [4, 768, 768], P('section'), may hold values from -1.75 to 1.75
- up_weight: bfloat16 [4, 768, 3072], P('section'), may hold values from -0.21875 to 0.21875
- down_weight: bfloat16 [4, 3072, 768], P('section'), may hold values from -0.109375 to 0.109375
- vectors: float32 [4, 9216], P('section'), may hold values from -1.5 to 1.5
- cotangent: bfloat16 [2, 8, 256, 768], P(None, 'dp'), may hold values from -6 to 6
Outputs:
- layer_outputs: bfloat16 [4, 2, 8, 256, 768], P('section', None, 'dp')
- input_grads: float32 [4, 2, 8, 256, 768], P('section', None, 'dp')
- qkv_grad: float32 [4, 768, 2304], P('section', 'dp')
- out_grad: float32 [4, 768, 768], P('section', 'dp')
- up_grad: float32 [4, 768, 3072], P('section', 'dp')
- down_grad: float32 [4, 3072, 768], P('section', 'dp')
- vector_grad: float32 [4, 9216], P('section', 'dp')
The draws below stay inside these ranges and needn't reach their ends.
Inputs may be any that keep to these rules, and one draw needn't show every extreme that they name: `lengths`: patches of a clip at positions from its length on are padding; some clip in every draw has exactly 256 valid patches.
All inputs are finite; a program needn't handle non-finite values.
Results may differ from the reference program's by a relative error of at most 0.012.
Values may be sent and summed in bfloat16 or wider, within the bound.
A program may use at most 512 MiB of HBM per device.

```python
import math
import jax
import jax.numpy as jnp
from jax import lax

D = 768
HEADS = 12
HEAD_DIM = 64
FF = 3072
LEN = 256
MICRO = 2
CLIPS = 8
LAYERS = 4


def draw_lengths(key, part):
    key = jax.random.fold_in(key, 11)
    draw_key, spot_key = jax.random.split(key)
    drawn = jax.random.randint(draw_key, (MICRO * CLIPS,), LEN // 5, LEN + 1)
    chosen = jax.random.randint(spot_key, (), 0, MICRO * CLIPS)
    drawn = jnp.where(jnp.arange(MICRO * CLIPS) == chosen, LEN, drawn)
    return drawn.reshape(MICRO, CLIPS).astype(jnp.int32)


def steps_of(key, dims, cuts, low, high):
    factor_of, own = 1.0, jax.random.fold_in(key, 6)
    for position, shards_of in cuts:
        steps = jnp.exp(jax.random.uniform(jax.random.fold_in(own, position), (shards_of,), jnp.float32, low / len(cuts), high / len(cuts)))
        factor_of = factor_of * jnp.repeat(steps, dims[position] // shards_of).reshape([-1 if axis == position else 1 for axis in range(len(dims))])
    return factor_of


def centred(key, extent, deviation, reach, cuts=(), held_as=jnp.bfloat16):
    level = steps_of(key, extent, cuts, -0.22, 0.18) if cuts else 1.0
    values = jax.random.normal(key, extent, jnp.float32) * deviation * level
    return jnp.minimum(jnp.maximum(values, -reach), reach).astype(held_as)


def setup_inputs(seed: int = 0) -> dict:
    streams_of = jax.random.split(jax.random.key(seed), 9)
    patches = centred(streams_of[0], (MICRO, CLIPS, LEN, D), 1.0, 6.0, ((1, 8),))
    lengths = draw_lengths(jax.random.fold_in(streams_of[8], 71), 0)
    qkv_weight = centred(streams_of[2], (LAYERS, D, 3 * D), D ** -0.5, 0.21875, ((0, 4),))
    out_weight = centred(streams_of[3], (LAYERS, D, D), (D // 64) ** -0.5, 1.75, ((0, 4),))
    up_weight = centred(streams_of[4], (LAYERS, D, FF), D ** -0.5, 0.21875, ((0, 4),))
    down_weight = centred(streams_of[5], (LAYERS, FF, D), FF ** -0.5, 0.109375, ((0, 4),))
    vectors = centred(streams_of[6], (LAYERS, 8 * D + FF), 0.3, 1.5, ((0, 4),), jnp.float32)
    cotangent = centred(streams_of[7], (MICRO, CLIPS, LEN, D), 1.0, 6.0, ((1, 8),))
    return {"patches": patches, "lengths": lengths, "qkv_weight": qkv_weight, "out_weight": out_weight, "up_weight": up_weight, "down_weight": down_weight, "vectors": vectors, "cotangent": cotangent}


@jax.custom_vjp
def low(v):
    return lax.optimization_barrier(v.astype(jnp.bfloat16)).astype(jnp.float32)

@jax.custom_vjp
def low_back(v):
    return v

def low_keep(v):
    return (low(v), None)

def low_pass(kept, grad):
    return (grad,)

def back_keep(v):
    return (v, None)

def back_low(kept, grad):
    return (low(grad),)
low.defvjp(low_keep, low_pass)
low_back.defvjp(back_keep, back_low)
EPS = 1e-06

def exact_dot(left, right):
    return jnp.dot(left, right, precision=lax.Precision.HIGHEST, preferred_element_type=jnp.float32)

def exact_einsum(form, left, right):
    return jnp.einsum(form, left, right, precision=lax.Precision.HIGHEST, preferred_element_type=jnp.float32)

def normed(hidden, gain, offset):
    average = lax.optimization_barrier(jnp.mean(hidden, axis=-1, keepdims=True))
    centered = hidden - average
    variance = lax.optimization_barrier(jnp.mean(centered * centered, axis=-1, keepdims=True))
    return centered * lax.rsqrt(variance + EPS) * (1.0 + gain) + offset

def layer_block(hidden, key_valid, qkv_weight, out_weight, up_weight, down_weight, vector):
    row_count = hidden.shape[0]
    feature_width = hidden.shape[1]
    pieces = [vector[piece_index * feature_width:(piece_index + 1) * feature_width] for piece_index in range(8)]
    gain_one, shift_one, bias_q, bias_v, bias_o, gain_two, shift_two, bias_d = pieces
    bias_u = vector[8 * feature_width:]
    normed_one = low(normed(hidden, gain_one, shift_one))
    projected = exact_dot(normed_one, qkv_weight)
    queries = low_back(low(projected[:, :feature_width] + bias_q)).reshape(row_count, HEADS, HEAD_DIM)
    key_heads = low_back(low(projected[:, feature_width:2 * feature_width])).reshape(row_count, HEADS, HEAD_DIM)
    value_heads = low_back(low(projected[:, 2 * feature_width:] + bias_v)).reshape(row_count, HEADS, HEAD_DIM)
    score_scale = 1.0 / math.sqrt(HEAD_DIM)
    scores = low_back(exact_einsum('qhd,khd->hqk', queries, key_heads) * score_scale)
    scores = jnp.where(key_valid[None, None, :], scores, -1e+30)
    soft_weights = low(jax.nn.softmax(scores, axis=-1))
    attended = low_back(low(exact_einsum('hqk,khd->qhd', soft_weights, value_heads).reshape(row_count, feature_width)))
    hidden_one = hidden + low_back(exact_dot(attended, out_weight) + bias_o)
    normed_two = low(normed(hidden_one, gain_two, shift_two))
    upward = low_back(exact_dot(normed_two, up_weight) + bias_u)
    activated = low(jax.nn.gelu(upward, approximate=False))
    return hidden_one + low_back(exact_dot(activated, down_weight) + bias_d)

def clip_outputs(inputs, nudges, key_valid, qkv_weight, out_weight, up_weight, down_weight, vectors):
    hidden = inputs + nudges[0]
    results = []
    for level in range(LAYERS):
        output = low(layer_block(hidden, key_valid, qkv_weight[level], out_weight[level], up_weight[level], down_weight[level], vectors[level]))
        results.append(output)
        if level + 1 < LAYERS:
            hidden = low_back(output) + nudges[level + 1]
    return jnp.stack(results)

def reference(patches, lengths, qkv_weight, out_weight, up_weight, down_weight, vectors, cotangent):
    micro_count = patches.shape[0]
    clip_count = patches.shape[1]
    row_count = patches.shape[2]
    feature_width = patches.shape[3]
    total = micro_count * clip_count
    inputs = patches.astype(jnp.float32).reshape(total, row_count, feature_width)
    key_valid = jnp.arange(row_count, dtype=jnp.int32)[None, :] < lengths.reshape(total, 1)
    nudges = jnp.zeros((total, LAYERS, row_count, feature_width), jnp.float32)
    weights = (qkv_weight.astype(jnp.float32), out_weight.astype(jnp.float32), up_weight.astype(jnp.float32), down_weight.astype(jnp.float32))

    def network(inputs, nudges, qkv_full, out_full, up_full, down_full, vector_full):

        def per_clip(items):
            return jax.checkpoint(clip_outputs)(items[0], items[1], items[2], qkv_full, out_full, up_full, down_full, vector_full)
        return lax.map(per_clip, (inputs, nudges, key_valid))
    outputs, pullback = jax.vjp(network, inputs, nudges, weights[0], weights[1], weights[2], weights[3], vectors)
    target = jnp.where(key_valid[:, :, None], cotangent.astype(jnp.float32).reshape(total, row_count, feature_width), 0.0)
    full_target = jnp.zeros_like(outputs).at[:, LAYERS - 1].set(target)
    gradients = pullback(full_target)
    layer_outputs = outputs.reshape(micro_count, clip_count, LAYERS, row_count, feature_width).transpose(2, 0, 1, 3, 4).astype(jnp.bfloat16)
    input_grads = gradients[1].reshape(micro_count, clip_count, LAYERS, row_count, feature_width).transpose(2, 0, 1, 3, 4)
    return (layer_outputs, input_grads, gradients[2], gradients[3], gradients[4], gradients[5], gradients[6])
```

```python
from functools import partial

import jax
import jax.numpy as jnp
from jax import lax
from jax.experimental import pallas as pl
from jax.experimental.pallas import tpu as pltpu
from jax.sharding import PartitionSpec as P

HEAD_DIM = 64
EPS = 1e-06
F32 = jnp.float32
BF16 = jnp.bfloat16
MESH = pl.DeviceIdType.MESH


def nn(left, right):
    return jnp.dot(left, right, preferred_element_type=F32)


def nt(left, right):
    return lax.dot_general(left, right, (((1,), (1,)), ((), ())), preferred_element_type=F32)


def tn(left, right):
    return lax.dot_general(left, right, (((0,), (0,)), ((), ())), preferred_element_type=F32)


def normalize(hidden):
    centered = hidden - jnp.mean(hidden, axis=-1, keepdims=True)
    inverse = lax.rsqrt(jnp.mean(centered * centered, axis=-1, keepdims=True) + EPS)
    return centered * inverse, inverse


def norm_back(grad, unit, inverse):
    average = jnp.mean(grad, axis=-1, keepdims=True)
    slope = jnp.mean(grad * unit, axis=-1, keepdims=True)
    return inverse * (grad - average - unit * slope)


def gelu_pair(u):
    phi = 0.5 + 0.5 * lax.erf(u * 0.7071067811865476)
    density = jnp.exp(u * u * -0.5) * 0.3989422804014327
    return u * phi, phi + u * density


class Refs:
    def __init__(self, names, refs):
        self.__dict__.update(zip(names, refs))


INPUTS = ("patches", "lengths", "wqkv_h", "wout_h", "wup_h", "wdown_h", "vec", "cot")
OUTPUTS = ("outputs", "input_grads", "gqkv", "gout", "gup", "gdown", "gvec")


def scratch_plan(micro, rows, width, hidden):
    heads = width // HEAD_DIM
    dma = pltpu.SemaphoreType.DMA
    vm = pltpu.VMEM
    act = vm((micro, rows, width), BF16)
    return dict(
        wqkv=vm((width, 3 * width), BF16),
        wout=vm((width, width), BF16),
        wup=vm((width, hidden), BF16),
        wdown=vm((hidden, width), BF16),
        x=act, a1=act, n1=act, o=act, n2=act, a2=act, y=act, e=act, eo=act, f=act,
        r1=vm((micro, rows, 128), F32),
        r2=vm((micro, rows, 128), F32),
        qkv=vm((micro, rows, 3 * width), BF16),
        bias=vm((1, 3 * width), F32),
        p=vm((micro, heads, rows, rows), BF16),
        rl=vm((micro, rows, width), F32),
        of=vm((micro, rows, width), F32),
        g=vm((micro, rows, hidden), BF16),
        gp=vm((micro, rows, hidden), BF16),
        du=vm((micro, rows, hidden), BF16),
        dp=vm((micro, rows, 3 * width), BF16),
        do=vm((rows, width), BF16),
        doo=vm((rows, width), BF16),
        rest=vm((rows, width), BF16),
        h1=vm((rows, width), F32),
        da=vm((rows, width), F32),
        ig=vm((micro, rows, width), F32),
        stage=vm((2, width, width), BF16),
        wsem=dma((4,)),
        psem=dma((micro,)),
        csem=dma((micro,)),
        xsend=dma((micro,)),
        xrecv=dma((micro,)),
        esend=dma((micro,)),
        erecv=dma((micro,)),
        osem=dma((micro,)),
        isem=dma((micro,)),
        gsem=dma((2,)),
    )


def pair_masks():
    lane = lax.broadcasted_iota(jnp.int32, (1, 128), 1)
    return (lane < HEAD_DIM).astype(BF16), (lane >= HEAD_DIM).astype(BF16), lane < HEAD_DIM


def forward_attention(k, m, key_bias, width):
    rows = k.x.shape[1]
    vec = k.vec
    unit, inverse = normalize(k.x[m].astype(F32))
    k.n1[m] = unit.astype(BF16)
    k.r1[m] = jnp.broadcast_to(inverse, (rows, 128))
    k.a1[m] = (unit * (1.0 + vec[:, :width]) + vec[:, width : 2 * width]).astype(BF16)
    normed = k.a1[m]
    for c in range(0, 3 * width, 256):
        k.qkv[m, :, c : c + 256] = (nn(normed, k.wqkv[:, c : c + 256]) + k.bias[:, c : c + 256]).astype(BF16)
    low, high, first = pair_masks()
    ones = jnp.ones((rows, 128), BF16)
    for c in range(0, width, 128):
        queries = k.qkv[m, :, c : c + 128]
        keys = k.qkv[m, :, width + c : width + c + 128]
        values = jnp.concatenate([k.qkv[m, :, 2 * width + c : 2 * width + c + 128], ones], axis=1)
        sums = []
        for half, mask in enumerate((low, high)):
            scores = nt(queries * (mask * jnp.asarray(HEAD_DIM**-0.5, BF16)), keys) + key_bias
            top = jnp.max(scores, axis=-1, keepdims=True)
            raised = jnp.exp(scores - top).astype(BF16)
            k.p[m, c // HEAD_DIM + half] = raised
            sums.append(nn(raised, values))
        inverse_sum = 1.0 / jnp.where(first, sums[0][:, 128:], sums[1][:, 128:])
        k.rl[m, :, c : c + 128] = inverse_sum
        joined = jnp.where(first, sums[0][:, :128], sums[1][:, :128]) * inverse_sum
        k.of[m, :, c : c + 128] = joined
        k.o[m, :, c : c + 128] = joined.astype(BF16)
    attended = k.o[m]
    for c in range(0, width, 256):
        k.h1[:, c : c + 256] = k.x[m, :, c : c + 256].astype(F32) + (
            nn(attended, k.wout[:, c : c + 256]) + vec[:, 4 * width + c : 4 * width + c + 256]
        )
    unit, inverse = normalize(k.h1[...])
    k.n2[m] = unit.astype(BF16)
    k.r2[m] = jnp.broadcast_to(inverse, (rows, 128))
    k.a2[m] = (unit * (1.0 + vec[:, 5 * width : 6 * width]) + vec[:, 6 * width : 7 * width]).astype(BF16)


def forward_mlp(k, m, width, hidden):
    vec = k.vec
    normed = k.a2[m]
    for c in range(0, hidden, 256):
        u = nn(normed, k.wup[:, c : c + 256]) + vec[:, 8 * width + c : 8 * width + c + 256]
        value, slope = gelu_pair(u)
        k.g[m, :, c : c + 256] = value.astype(BF16)
        k.gp[m, :, c : c + 256] = slope.astype(BF16)
    activated = k.g[m]
    k.y[m] = (k.h1[...] + (nn(activated, k.wdown[...]) + vec[:, 7 * width : 8 * width])).astype(BF16)


def add_vector(k, at, value):
    k.gvec[:, at : at + value.shape[1]] += value


def backward_chain(k, m, width, hidden):
    rows = k.x.shape[1]
    vec = k.vec
    grad = k.e[m]
    for c in range(0, hidden, 256):
        k.du[m, :, c : c + 256] = (
            nt(grad, k.wdown[c : c + 256, :]) * k.gp[m, :, c : c + 256].astype(F32)
        ).astype(BF16)
    grad_two = nt(k.du[m], k.wup[...])
    unit = k.n2[m].astype(F32)
    add_vector(k, 5 * width, jnp.sum(grad_two * unit, axis=0, keepdims=True))
    add_vector(k, 6 * width, jnp.sum(grad_two, axis=0, keepdims=True))
    grad_mid = k.e[m].astype(F32) + norm_back(
        grad_two * (1.0 + vec[:, 5 * width : 6 * width]), unit, k.r2[m, :, :1]
    )
    k.h1[...] = grad_mid
    k.f[m] = grad_mid.astype(BF16)
    branch = k.f[m]
    k.do[...] = (nt(branch, k.wout[...]) * k.rl[m]).astype(BF16)
    product = k.do[...].astype(F32) * k.of[m]
    k.doo[...] = product.astype(BF16)
    k.rest[...] = (product - k.doo[...].astype(F32)).astype(BF16)
    low, high, first = pair_masks()
    minus = jnp.full((rows, 128), -1.0, BF16)
    scale = HEAD_DIM**-0.5
    for c in range(0, width, 128):
        queries = k.qkv[m, :, c : c + 128]
        keys = k.qkv[m, :, width + c : width + c + 128]
        values = jnp.concatenate([k.qkv[m, :, 2 * width + c : 2 * width + c + 128], minus], axis=1)
        grads = k.do[:, c : c + 128]
        inner = k.doo[:, c : c + 128]
        rest = pltpu.roll(k.rest[:, c : c + 128].astype(F32), HEAD_DIM, 1).astype(BF16)
        inners = (jnp.where(first, inner, rest), jnp.where(first, rest, inner))
        total_q = total_k = total_v = 0.0
        for half, mask in enumerate((low, high)):
            raised = k.p[m, c // HEAD_DIM + half]
            left = jnp.concatenate([grads * mask, inners[half]], axis=1)
            grad_scores = (raised.astype(F32) * nt(left, values)).astype(BF16)
            total_v = total_v + tn(raised, grads * mask)
            total_q = total_q + nn(grad_scores, keys * mask)
            total_k = total_k + tn(grad_scores, queries * mask)
        k.dp[m, :, c : c + 128] = (total_q * scale).astype(BF16)
        k.dp[m, :, width + c : width + c + 128] = (total_k * scale).astype(BF16)
        k.dp[m, :, 2 * width + c : 2 * width + c + 128] = total_v.astype(BF16)
    grad_one = nt(k.dp[m], k.wqkv[...])
    unit = k.n1[m].astype(F32)
    add_vector(k, 0, jnp.sum(grad_one * unit, axis=0, keepdims=True))
    add_vector(k, width, jnp.sum(grad_one, axis=0, keepdims=True))
    grad_in = k.h1[...] + norm_back(grad_one * (1.0 + vec[:, :width]), unit, k.r1[m, :, :1])
    k.ig[m] = grad_in
    k.eo[m] = grad_in.astype(BF16)


def pipeline_kernel(scratch_names, *refs):
    k = Refs(INPUTS + OUTPUTS + scratch_names, refs)
    sec = lax.axis_index("section")
    count = lax.axis_size("section")
    micro, rows, width = k.x.shape
    hidden = k.wup.shape[1]
    is_first = sec == 0
    is_last = sec == count - 1
    after = jnp.minimum(sec + 1, count - 1)
    before = jnp.maximum(sec - 1, 0)

    barrier = pltpu.get_barrier_semaphore()

    @pl.when(sec > 0)
    def _():
        pl.semaphore_signal(barrier, inc=1, device_id={"section": before}, device_id_type=MESH)

    @pl.when(sec < count - 1)
    def _():
        pl.semaphore_signal(barrier, inc=1, device_id={"section": after}, device_id_type=MESH)

    def patch_copy(m):
        return pltpu.make_async_copy(k.patches.at[m], k.x.at[m], k.psem.at[m])

    def cot_copy(m):
        return pltpu.make_async_copy(k.cot.at[m], k.e.at[m], k.csem.at[m])

    loads = [
        pltpu.make_async_copy(src.at[0], dst, k.wsem.at[i])
        for i, (src, dst) in enumerate(
            ((k.wqkv_h, k.wqkv), (k.wout_h, k.wout), (k.wup_h, k.wup), (k.wdown_h, k.wdown))
        )
    ]

    @pl.when(is_first)
    def _():
        for m in range(micro):
            patch_copy(m).start()

    for load in loads:
        load.start()

    @pl.when(is_last)
    def _():
        for m in range(micro):
            cot_copy(m).start()

    k.bias[:, : width] = k.vec[:, 2 * width : 3 * width]
    k.bias[:, width : 2 * width] = jnp.zeros((1, width), F32)
    k.bias[:, 2 * width :] = k.vec[:, 3 * width : 4 * width]
    k.gvec[...] = jnp.zeros_like(k.gvec)
    loads[0].wait()
    loads[1].wait()

    def y_send(m):
        return pltpu.make_async_remote_copy(
            src_ref=k.y.at[m], dst_ref=k.x.at[m], send_sem=k.xsend.at[m], recv_sem=k.xrecv.at[m],
            device_id={"section": after}, device_id_type=MESH,
        )

    def e_send(m):
        return pltpu.make_async_remote_copy(
            src_ref=k.eo.at[m], dst_ref=k.e.at[m], send_sem=k.esend.at[m], recv_sem=k.erecv.at[m],
            device_id={"section": before}, device_id_type=MESH,
        )

    def out_copy(m):
        return pltpu.make_async_copy(k.y.at[m], k.outputs.at[m], k.osem.at[m])

    def in_copy(m):
        return pltpu.make_async_copy(k.ig.at[m], k.input_grads.at[m], k.isem.at[m])

    pl.semaphore_wait(
        barrier, (sec > 0).astype(jnp.int32) + (sec < count - 1).astype(jnp.int32)
    )

    def forward_step(m, carry):
        @pl.when(is_first)
        def _():
            patch_copy(m).wait()

        @pl.when(sec > 0)
        def _():
            y_send(m).wait_recv()

        key_bias = jnp.where(
            lax.broadcasted_iota(jnp.int32, (1, rows), 1) < k.lengths[m, 0], 0.0, -1e30
        )
        forward_attention(k, m, key_bias, width)

        @pl.when(m == 0)
        def _():
            loads[2].wait()
            loads[3].wait()

        forward_mlp(k, m, width, hidden)

        @pl.when(sec < count - 1)
        def _():
            y_send(m).start()

        out_copy(m).start()
        return carry

    lax.fori_loop(0, micro, forward_step, 0)

    def backward_step(m, carry):
        @pl.when(is_last)
        def _():
            cot_copy(m).wait()
            valid = lax.broadcasted_iota(jnp.int32, (rows, width), 0) < k.lengths[m, 0]
            k.e[m] = jnp.where(valid, k.e[m].astype(F32), 0.0).astype(BF16)

        @pl.when(sec < count - 1)
        def _():
            e_send(m).wait_recv()

        backward_chain(k, m, width, hidden)

        @pl.when(sec > 0)
        def _():
            e_send(m).start()

        in_copy(m).start()
        return carry

    lax.fori_loop(0, micro, backward_step, 0)

    both = micro * rows
    ones = jnp.ones((16, both), BF16)

    def joined(ref, *at):
        return ref[at if at else ...].reshape(both, -1)

    def column_sums(value):
        return nn(ones, value)[:1]

    pending = [None, None]
    turn = 0

    def emit(value, target):
        nonlocal turn
        slot = turn % 2
        if pending[slot] is not None:
            pending[slot].wait()
        k.stage[slot] = value.astype(BF16)
        copy = pltpu.make_async_copy(k.stage.at[slot], target, k.gsem.at[slot])
        copy.start()
        pending[slot] = copy
        turn += 1

    add_vector(k, 7 * width, column_sums(joined(k.e)))
    add_vector(k, 4 * width, column_sums(joined(k.f)))
    for c in range(0, hidden, width):
        grads = k.du[:, :, c : c + width].reshape(both, width)
        emit(tn(joined(k.a2), grads), k.gup.at[:, pl.ds(c, width)])
        add_vector(k, 8 * width + c, column_sums(grads))
    for c in range(0, hidden, width):
        emit(tn(k.g[:, :, c : c + width].reshape(both, width), joined(k.e)), k.gdown.at[pl.ds(c, width)])
    for part in range(3):
        c = part * width
        grads = k.dp[:, :, c : c + width].reshape(both, width)
        emit(tn(joined(k.a1), grads), k.gqkv.at[:, pl.ds(c, width)])
        if part != 1:
            add_vector(k, (2 if part == 0 else 3) * width, column_sums(grads))
    emit(tn(joined(k.o), joined(k.f)), k.gout)
    for copy in pending:
        copy.wait()
    for m in range(micro):
        out_copy(m).wait()
        in_copy(m).wait()

        @pl.when(sec < count - 1)
        def _():
            y_send(m).wait_send()

        @pl.when(sec > 0)
        def _():
            e_send(m).wait_send()


def shards(patches, lengths, qkv_weight, out_weight, up_weight, down_weight, vectors, cotangent):
    micro, _, rows, width = patches.shape
    hidden = up_weight.shape[2]
    plan = scratch_plan(micro, rows, width, hidden)
    anywhere = pl.BlockSpec(memory_space=pl.ANY)
    in_vmem = pl.BlockSpec(memory_space=pltpu.VMEM)
    results = pl.pallas_call(
        partial(pipeline_kernel, tuple(plan)),
        out_shape=(
            jax.ShapeDtypeStruct((micro, rows, width), BF16),
            jax.ShapeDtypeStruct((micro, rows, width), F32),
            jax.ShapeDtypeStruct((width, 3 * width), BF16),
            jax.ShapeDtypeStruct((width, width), BF16),
            jax.ShapeDtypeStruct((width, hidden), BF16),
            jax.ShapeDtypeStruct((hidden, width), BF16),
            jax.ShapeDtypeStruct(vectors.shape, F32),
        ),
        in_specs=[
            anywhere,
            pl.BlockSpec(memory_space=pltpu.SMEM),
            anywhere,
            anywhere,
            anywhere,
            anywhere,
            in_vmem,
            anywhere,
        ],
        out_specs=(anywhere,) * 6 + (in_vmem,),
        scratch_shapes=list(plan.values()),
        compiler_params=pltpu.CompilerParams(
            collective_id=0, has_side_effects=True, vmem_limit_bytes=60 << 20
        ),
    )(
        patches[:, 0],
        lengths,
        qkv_weight,
        out_weight,
        up_weight,
        down_weight,
        vectors,
        cotangent[:, 0],
    )
    outputs, input_grads, *grads, vector_grad = results
    collected = [
        lax.psum_scatter(grad[None], "dp", scatter_dimension=1, tiled=True).astype(F32)
        for grad in grads
    ]
    return (
        outputs[None, :, None],
        input_grads[None, :, None],
        *collected,
        lax.psum_scatter(vector_grad, "dp", scatter_dimension=1, tiled=True),
    )


def solution(mesh):
    placed = (
        P(None, "dp", None, None),
        P(None, "dp"),
        P("section", None, None),
        P("section", None, None),
        P("section", None, None),
        P("section", None, None),
        P("section", None),
        P(None, "dp", None, None),
    )
    return jax.shard_map(
        shards,
        mesh=mesh,
        in_specs=placed,
        out_specs=(
            P("section", None, "dp", None, None),
            P("section", None, "dp", None, None),
            P("section", "dp", None),
            P("section", "dp", None),
            P("section", "dp", None),
            P("section", "dp", None),
            P("section", "dp"),
        ),
        check_vma=False,
    )
```

```python
from functools import partial

import jax
import jax.numpy as jnp
from jax import lax
from jax.experimental import pallas as pl
from jax.experimental.pallas import tpu as pltpu
from jax.sharding import PartitionSpec as P

HEAD_DIM = 64
EPS = 1e-06
F32 = jnp.float32
BF16 = jnp.bfloat16
MESH = pl.DeviceIdType.MESH


def nn(left, right):
    return jnp.dot(left, right, preferred_element_type=F32)


def nt(left, right):
    return lax.dot_general(left, right, (((1,), (1,)), ((), ())), preferred_element_type=F32)


def tn(left, right):
    return lax.dot_general(left, right, (((0,), (0,)), ((), ())), preferred_element_type=F32)


def normalize(hidden):
    centered = hidden - jnp.mean(hidden, axis=-1, keepdims=True)
    inverse = lax.rsqrt(jnp.mean(centered * centered, axis=-1, keepdims=True) + EPS)
    return centered * inverse, inverse


def norm_back(grad, unit, inverse):
    average = jnp.mean(grad, axis=-1, keepdims=True)
    slope = jnp.mean(grad * unit, axis=-1, keepdims=True)
    return inverse * (grad - average - unit * slope)


def gelu_pair(u):
    phi = 0.5 + 0.5 * lax.erf(u * 0.7071067811865476)
    density = jnp.exp(u * u * -0.5) * 0.3989422804014327
    return u * phi, phi + u * density


class Refs:
    def __init__(self, names, refs):
        self.__dict__.update(zip(names, refs))


INPUTS = ("patches", "lengths", "wqkv_h", "wout_h", "wup_h", "wdown_h", "vec", "cot")
RESULTS = ("outputs", "input_grads", "qkv_grad", "out_grad", "up_grad", "down_grad", "vector_grad")


def scratch_plan(micro, rows, width, hidden, chips, peers, fused):
    heads = width // HEAD_DIM
    dma = pltpu.SemaphoreType.DMA
    vm = pltpu.VMEM
    act = vm((micro, rows, width), BF16)
    blocks = vm((micro, chips, rows, width), BF16)
    plan = dict(
        wqkv=vm((width, 3 * width), BF16),
        wout=vm((width, width), BF16),
        wup=vm((width, hidden), BF16),
        wdown=vm((hidden, width), BF16),
        x=act, a1=act, n1=act, o=act, n2=act, y=act, a2=blocks, e=blocks,
        r1=vm((micro, rows, 128), F32),
        r2=vm((micro, rows, 128), F32),
        qkv=vm((micro, rows, 3 * width), BF16),
        bias=vm((1, 3 * width), F32),
        p=vm((micro, heads, rows, rows), BF16),
        wide=vm((rows, hidden), BF16),
        gp=vm((micro, rows, hidden), BF16),
        dp=vm((micro, rows, 3 * width), BF16),
        do=vm((rows, width), BF16),
        doo=vm((rows, width), BF16),
        rest=vm((rows, width), BF16),
        pool=vm((2 * width, width), F32),
        ig=vm((micro, rows, width), F32),
        wsem=dma((4,)),
        psem=dma((micro,)),
        csem=dma((micro,)),
        xsend=dma((micro,)),
        xrecv=dma((micro,)),
        esend=dma((micro,)),
        erecv=dma((micro,)),
        osem=dma((micro,)),
        isem=dma((micro,)),
        gsem=dma((3 * chips,)),
    )
    if fused:
        share = width // peers
        plan.update(
            gvec=vm((1, 8 * width + hidden), F32),
            asend=dma((2, micro, chips)),
            arecv=dma((micro, chips)),
            bsend=dma((2, micro, chips)),
            brecv=dma((micro, chips)),
            prx=vm((4, chips, share, width), BF16),
            pxsend=dma((4, chips)),
            pxrecv=dma((4, chips)),
            rsx=vm((2, 4, chips - 1, share, width), BF16),
            rsend=dma((2, 4, chips)),
            rrecv=dma((2, 4, chips)),
            vrx=vm((peers, 1, (8 * width + hidden) // peers), F32),
            vsend=dma((peers,)),
            vrecv=dma((peers,)),
            upx=vm((chips, 2, share, width), BF16),
            uprx=vm((chips, share, width), BF16),
            upsem=dma((2,)),
            dnx=vm((hidden // peers, width), BF16),
            dnrx=vm((hidden // peers, width), BF16),
            dnsem=dma((2,)),
            uax=vm((chips, share, width), BF16),
            uasend=dma((chips,)),
            uarecv=dma((chips,)),
        )
    return plan


def pair_masks():
    lane = lax.broadcasted_iota(jnp.int32, (1, 128), 1)
    return (lane < HEAD_DIM).astype(BF16), (lane >= HEAD_DIM).astype(BF16), lane < HEAD_DIM


def pool_rows(k, block, m=0):
    rows = k.x.shape[1]
    return pl.ds(pl.multiple_of((block + m) * rows, rows), rows)


RL, OF, MID = 0, 2, 4


def forward_attention(k, m, z, key_bias):
    rows, width = k.x.shape[1:]
    vec = k.vec
    unit, inverse = normalize(k.x[m].astype(F32))
    k.n1[m] = unit.astype(BF16)
    k.r1[m] = jnp.broadcast_to(inverse, (rows, 128))
    k.a1[m] = (unit * (1.0 + vec[:, :width]) + vec[:, width : 2 * width]).astype(BF16)
    normed = k.a1[m]
    for c in range(0, 3 * width, 256):
        k.qkv[m, :, c : c + 256] = (nn(normed, k.wqkv[:, c : c + 256]) + k.bias[:, c : c + 256]).astype(BF16)
    low, high, first = pair_masks()
    ones = jnp.ones((rows, 128), BF16)
    for c in range(0, width, 128):
        queries = k.qkv[m, :, c : c + 128]
        keys = k.qkv[m, :, width + c : width + c + 128]
        values = jnp.concatenate([k.qkv[m, :, 2 * width + c : 2 * width + c + 128], ones], axis=1)
        sums = []
        for half, mask in enumerate((low, high)):
            scores = nt(queries * (mask * jnp.asarray(HEAD_DIM**-0.5, BF16)), keys) + key_bias
            top = jnp.max(scores, axis=-1, keepdims=True)
            raised = jnp.exp(scores - top).astype(BF16)
            k.p[m, c // HEAD_DIM + half] = raised
            sums.append(nn(raised, values))
        inverse_sum = 1.0 / jnp.where(first, sums[0][:, 128:], sums[1][:, 128:])
        k.pool[pool_rows(k, RL, m), c : c + 128] = inverse_sum
        joined = jnp.where(first, sums[0][:, :128], sums[1][:, :128]) * inverse_sum
        k.pool[pool_rows(k, OF, m), c : c + 128] = joined
        k.o[m, :, c : c + 128] = joined.astype(BF16)
    attended = k.o[m]
    mid = pool_rows(k, MID)
    for c in range(0, width, 256):
        k.pool[mid, c : c + 256] = k.x[m, :, c : c + 256].astype(F32) + (
            nn(attended, k.wout[:, c : c + 256]) + vec[:, 4 * width + c : 4 * width + c + 256]
        )
    unit, inverse = normalize(k.pool[mid, :])
    k.n2[m] = unit.astype(BF16)
    k.r2[m] = jnp.broadcast_to(inverse, (rows, 128))
    k.a2[m, z] = (unit * (1.0 + vec[:, 5 * width : 6 * width]) + vec[:, 6 * width : 7 * width]).astype(BF16)


def forward_mlp(k, m, z):
    width = k.x.shape[2]
    vec = k.vec
    normed = k.a2[m, z]
    for c in range(0, k.wup.shape[1], 256):
        u = nn(normed, k.wup[:, c : c + 256]) + vec[:, 8 * width + c : 8 * width + c + 256]
        value, slope = gelu_pair(u)
        k.wide[:, c : c + 256] = value.astype(BF16)
        k.gp[m, :, c : c + 256] = slope.astype(BF16)
    added = nn(k.wide[...], k.wdown[...]) + vec[:, 7 * width : 8 * width]
    k.y[m] = (k.pool[pool_rows(k, MID), :] + added).astype(BF16)


def add_sums(ref, at, value):
    ref[:, at : at + value.shape[1]] += jnp.sum(value, axis=0, keepdims=True)


def backward_mlp(k, gvec, m, z):
    width = k.x.shape[2]
    vec = k.vec
    grad = k.e[m, z]
    add_sums(gvec, 7 * width, grad.astype(F32))
    for c in range(0, k.wup.shape[1], 256):
        grad_up = (
            nt(grad, k.wdown[c : c + 256, :]) * k.gp[m, :, c : c + 256].astype(F32)
        ).astype(BF16)
        k.wide[:, c : c + 256] = grad_up
        add_sums(gvec, 8 * width + c, grad_up.astype(F32))
    grad_two = nt(k.wide[...], k.wup[...])
    unit = k.n2[m].astype(F32)
    add_sums(gvec, 5 * width, grad_two * unit)
    add_sums(gvec, 6 * width, grad_two)
    grad_mid = k.e[m, z].astype(F32) + norm_back(
        grad_two * (1.0 + vec[:, 5 * width : 6 * width]), unit, k.r2[m, :, :1]
    )
    k.pool[pool_rows(k, MID), :] = grad_mid
    branch = grad_mid.astype(BF16)
    k.x[m] = branch
    add_sums(gvec, 4 * width, branch.astype(F32))


def backward_attention(k, gvec, m):
    rows, width = k.x.shape[1:]
    vec = k.vec
    k.do[...] = (nt(k.x[m], k.wout[...]) * k.pool[pool_rows(k, RL, m), :]).astype(BF16)
    product = k.do[...].astype(F32) * k.pool[pool_rows(k, OF, m), :]
    k.doo[...] = product.astype(BF16)
    k.rest[...] = (product - k.doo[...].astype(F32)).astype(BF16)
    low, high, first = pair_masks()
    minus = jnp.full((rows, 128), -1.0, BF16)
    scale = HEAD_DIM**-0.5
    for c in range(0, width, 128):
        queries = k.qkv[m, :, c : c + 128]
        keys = k.qkv[m, :, width + c : width + c + 128]
        values = jnp.concatenate([k.qkv[m, :, 2 * width + c : 2 * width + c + 128], minus], axis=1)
        grads = k.do[:, c : c + 128]
        inner = k.doo[:, c : c + 128]
        rest = pltpu.roll(k.rest[:, c : c + 128].astype(F32), HEAD_DIM, 1).astype(BF16)
        inners = (jnp.where(first, inner, rest), jnp.where(first, rest, inner))
        total_q = total_k = total_v = 0.0
        for half, mask in enumerate((low, high)):
            raised = k.p[m, c // HEAD_DIM + half]
            left = jnp.concatenate([grads * mask, inners[half]], axis=1)
            grad_scores = (raised.astype(F32) * nt(left, values)).astype(BF16)
            total_v = total_v + tn(raised, grads * mask)
            total_q = total_q + nn(grad_scores, keys * mask)
            total_k = total_k + tn(grad_scores, queries * mask)
        grad_q = (total_q * scale).astype(BF16)
        grad_v = total_v.astype(BF16)
        k.dp[m, :, c : c + 128] = grad_q
        k.dp[m, :, width + c : width + c + 128] = (total_k * scale).astype(BF16)
        k.dp[m, :, 2 * width + c : 2 * width + c + 128] = grad_v
        add_sums(gvec, 2 * width + c, grad_q.astype(F32))
        add_sums(gvec, 3 * width + c, grad_v.astype(F32))
    grad_one = nt(k.dp[m], k.wqkv[...])
    unit = k.n1[m].astype(F32)
    add_sums(gvec, 0, grad_one * unit)
    add_sums(gvec, width, grad_one)
    grad_in = k.pool[pool_rows(k, MID), :] + norm_back(
        grad_one * (1.0 + vec[:, :width]), unit, k.r1[m, :, :1]
    )
    k.ig[m] = grad_in
    k.y[m] = grad_in.astype(BF16)


def attention_weight_grads(k, after_chunk):
    micro, rows, width = k.x.shape
    both = micro * rows
    normed = k.a1[...].reshape(both, width)
    for part in range(3):
        grads = k.dp[:, :, part * width : (part + 1) * width].reshape(both, width)
        k.wqkv[:, part * width : (part + 1) * width] = tn(normed, grads).astype(BF16)
        after_chunk(part)
    k.wout[...] = tn(k.o[...].reshape(both, width), k.x[...].reshape(both, width)).astype(BF16)
    after_chunk(3)


def mlp_weight_grads(k, origin, start, fresh):
    micro, rows, width = k.x.shape
    both = micro * rows
    normed = k.a2[:, origin].reshape(both, width)
    grad = k.e[:, origin].reshape(both, width)
    for c in range(0, width, 256):
        at = pl.ds(pl.multiple_of(start + c, 256), 256)
        u = nn(normed, k.wup[:, at]) + k.vec[:, pl.ds(pl.multiple_of(8 * width + start + c, 256), 256)]
        value, slope = gelu_pair(u)
        grad_up = (nt(grad, k.wdown[at, :]) * slope).astype(BF16)
        up = tn(normed, grad_up)
        down = tn(value.astype(BF16), grad)
        if fresh:
            k.pool[:width, c : c + 256] = up
            k.pool[width + c : width + c + 256, :] = down
        else:
            k.pool[:width, c : c + 256] += up
            k.pool[width + c : width + c + 256, :] += down


def pipeline_kernel(scratch_names, fused, *refs):
    k = Refs(INPUTS + RESULTS + scratch_names, refs)
    sec = lax.axis_index("section")
    count = lax.axis_size("section")
    peers = lax.axis_size("dp")
    me = lax.axis_index("dp")
    micro, rows, width = k.x.shape
    hidden = k.wup.shape[1]
    chips = k.e.shape[1]
    z, core = (me // 2, me % 2) if fused else (0, 0)
    gvec = k.gvec if fused else k.vector_grad
    share = width // peers
    is_first = sec == 0
    is_last = sec == count - 1
    not_last = sec < count - 1
    after = jnp.minimum(sec + 1, count - 1)
    before = jnp.maximum(sec - 1, 0)

    barrier = pltpu.get_barrier_semaphore()

    @pl.when(sec > 0)
    def _():
        pl.semaphore_signal(barrier, inc=1, device_id={"section": before}, device_id_type=MESH)

    @pl.when(not_last)
    def _():
        pl.semaphore_signal(barrier, inc=1, device_id={"section": after}, device_id_type=MESH)

    if fused:
        for step in range(1, peers):
            pl.semaphore_signal(
                barrier, inc=1, device_id={"dp": (me + step) % peers}, device_id_type=MESH
            )

    def patch_copy(m):
        return pltpu.make_async_copy(k.patches.at[m], k.x.at[m], k.psem.at[m])

    def cot_copy(m):
        return pltpu.make_async_copy(k.cot.at[m], k.e.at[m, z], k.csem.at[m])

    loads = [
        pltpu.make_async_copy(src.at[0], dst, k.wsem.at[i])
        for i, (src, dst) in enumerate(
            ((k.wqkv_h, k.wqkv), (k.wout_h, k.wout), (k.wup_h, k.wup), (k.wdown_h, k.wdown))
        )
    ]

    @pl.when(is_first)
    def _():
        for m in range(micro):
            patch_copy(m).start()

    for load in loads:
        load.start()

    @pl.when(is_last)
    def _():
        for m in range(micro):
            cot_copy(m).start()

    k.bias[:, :width] = k.vec[:, 2 * width : 3 * width]
    k.bias[:, width : 2 * width] = jnp.zeros((1, width), F32)
    k.bias[:, 2 * width :] = k.vec[:, 3 * width : 4 * width]
    gvec[...] = jnp.zeros_like(gvec)
    loads[0].wait()
    loads[1].wait()

    def y_send(m):
        return pltpu.make_async_remote_copy(
            src_ref=k.y.at[m], dst_ref=k.x.at[m], send_sem=k.xsend.at[m], recv_sem=k.xrecv.at[m],
            device_id={"section": after}, device_id_type=MESH,
        )

    def e_send(m):
        return pltpu.make_async_remote_copy(
            src_ref=k.y.at[m], dst_ref=k.e.at[m, z], send_sem=k.esend.at[m], recv_sem=k.erecv.at[m],
            device_id={"section": before}, device_id_type=MESH,
        )

    def out_copy(m):
        return pltpu.make_async_copy(k.y.at[m], k.outputs.at[m], k.osem.at[m])

    def in_copy(m):
        return pltpu.make_async_copy(k.ig.at[m], k.input_grads.at[m], k.isem.at[m])

    def to_peer(src, dst, send, recv, device):
        return pltpu.make_async_remote_copy(
            src_ref=src, dst_ref=dst, send_sem=send, recv_sem=recv,
            device_id={"dp": device}, device_id_type=MESH,
        )

    def pass_on(ref, sends, recvs, m, origin, up):
        return to_peer(
            ref.at[m, origin], ref.at[m, origin], sends.at[0 if up else 1, m, origin],
            recvs.at[m, origin], me + 2 if up else me - 2,
        )

    def share_own(ref, sends, recvs, m):
        @pl.when(z < chips - 1)
        def _():
            pass_on(ref, sends, recvs, m, z, True).start()

        @pl.when(z > 0)
        def _():
            pass_on(ref, sends, recvs, m, z, False).start()

    def relay(ref, sends, recvs, m, distance):
        @pl.when(z >= distance)
        def _():
            pass_on(ref, sends, recvs, m, z - distance, True).wait_recv()

            @pl.when(z < chips - 1)
            def _():
                pass_on(ref, sends, recvs, m, z - distance, True).start()

        @pl.when(z + distance < chips)
        def _():
            pass_on(ref, sends, recvs, m, z + distance, False).wait_recv()

            @pl.when(z > 0)
            def _():
                pass_on(ref, sends, recvs, m, z + distance, False).start()

    def settle(ref, sends, recvs, m):
        for distance in range(chips):
            @pl.when((z >= distance) & (z < chips - 1))
            def _():
                pass_on(ref, sends, recvs, m, z - distance, True).wait_send()

            @pl.when((z + distance < chips) & (z > 0))
            def _():
                pass_on(ref, sends, recvs, m, z + distance, False).wait_send()

    if fused:
        acts = (k.a2, k.asend, k.arecv)
        errs = (k.e, k.bsend, k.brecv)
    arrivals = (sec > 0).astype(jnp.int32) + not_last.astype(jnp.int32)
    pl.semaphore_wait(barrier, arrivals + (peers - 1 if fused else 0))

    @pl.when(is_last)
    def _():
        for m in range(micro):
            cot_copy(m).wait()
            valid = lax.broadcasted_iota(jnp.int32, (rows, width), 0) < k.lengths[m, 0]
            k.e[m, z] = jnp.where(valid, k.e[m, z].astype(F32), 0.0).astype(BF16)
            if fused:
                share_own(*errs, m)
        if fused:
            for distance in range(1, chips - 1):
                for m in range(micro):
                    relay(*errs, m, distance)

    def forward_step(m, carry):
        @pl.when(is_first)
        def _():
            patch_copy(m).wait()

        @pl.when(sec > 0)
        def _():
            y_send(m).wait_recv()

        key_bias = jnp.where(
            lax.broadcasted_iota(jnp.int32, (1, rows), 1) < k.lengths[m, 0], 0.0, -1e30
        )
        forward_attention(k, m, z, key_bias)
        if fused:
            share_own(*acts, m)

        @pl.when(m == 0)
        def _():
            loads[2].wait()
            loads[3].wait()

        forward_mlp(k, m, z)

        @pl.when(not_last)
        def _():
            y_send(m).start()

        out_copy(m).start()
        return carry

    lax.fori_loop(0, micro, forward_step, 0)

    def relay_acts():
        for distance in range(1, chips - 1):
            for m in range(micro):
                relay(*acts, m, distance)

    if fused:
        pl.when(not_last)(relay_acts)

    for m in range(micro):
        out_copy(m).wait()

        @pl.when(not_last)
        def _():
            y_send(m).wait_send()

    def backward_step(m, carry):
        @pl.when(not_last)
        def _():
            e_send(m).wait_recv()
            if fused:
                share_own(*errs, m)

        backward_mlp(k, gvec, m, z)
        if fused:
            @pl.when(not_last & (m == micro - 1))
            def _():
                for early in range(micro - 1):
                    relay(*errs, early, 1)

        backward_attention(k, gvec, m)

        @pl.when(sec > 0)
        def _():
            e_send(m).start()

        in_copy(m).start()
        return carry

    lax.fori_loop(0, micro, backward_step, 0)

    def finish_hops():
        for m in range(micro):
            in_copy(m).wait()

            @pl.when(sec > 0)
            def _():
                e_send(m).wait_send()

    if not fused:
        attention_weight_grads(k, lambda part: None)
        for c in range(0, hidden, width):
            mlp_weight_grads(k, 0, c, True)
            k.wup[:, c : c + width] = k.pool[:width, :].astype(BF16)
            k.wdown[c : c + width, :] = k.pool[width:, :].astype(BF16)
        copies = [
            pltpu.make_async_copy(src, dst, k.wsem.at[i])
            for i, (src, dst) in enumerate(
                ((k.wqkv, k.qkv_grad), (k.wout, k.out_grad), (k.wup, k.up_grad), (k.wdown, k.down_grad))
            )
        ]
        for copy in copies:
            copy.start()
        for copy in copies:
            copy.wait()
        finish_hops()
        return

    sibling = me + 1 - 2 * core

    def part_rows(chip, parity):
        return pl.ds(pl.multiple_of(share * (2 * chip + parity), share), share)

    def part_ref(part, chip, parity):
        if part < 3:
            return k.wqkv.at[part_rows(chip, parity), pl.ds(part * width, width)]
        return k.wout.at[part_rows(chip, parity), :]

    def pair_copy(part, chip):
        return to_peer(
            part_ref(part, chip, 1 - core), k.prx.at[part, chip],
            k.pxsend.at[part, chip], k.pxrecv.at[part, chip], sibling,
        )

    def send_pair(part):
        for chip in range(chips):
            pair_copy(part, chip).start()

    attention_weight_grads(k, send_pair)

    length = gvec.shape[1] // peers

    def vector_copy(step):
        device = (me + step) % peers
        return to_peer(
            gvec.at[:, pl.ds(pl.multiple_of(device * length, 128), length)], k.vrx.at[step],
            k.vsend.at[step], k.vrecv.at[step], device,
        )

    for step in range(1, peers):
        vector_copy(step).start()

    def chain_copy(up, part, place):
        chip = place if up else chips - 1 - place
        lane = 0 if up else 1
        return to_peer(
            part_ref(part, chip, core), k.rsx.at[lane, part, place - 1],
            k.rsend.at[lane, part, place], k.rrecv.at[lane, part, place],
            me + 2 if up else me - 2,
        )

    def chain(stage, part):
        for up in (True, False):
            @pl.when((z if up else chips - 1 - z) == stage)
            def _():
                for place in range(chips - 1, stage, -1):
                    if stage > 0:
                        chain_copy(up, part, place).wait_recv()
                        chip = place if up else chips - 1 - place
                        target = part_ref(part, chip, core)
                        target[...] = (
                            target[...].astype(F32)
                            + k.rsx[0 if up else 1, part, place - 1].astype(F32)
                        ).astype(BF16)
                    chain_copy(up, part, place).start()

    for part in range(4):
        for chip in range(chips):
            pair_copy(part, chip).wait()
            target = part_ref(part, chip, core)
            target[...] = (target[...].astype(F32) + k.prx[part, chip].astype(F32)).astype(BF16)
        chain(0, part)

    @pl.when(not_last)
    def _():
        relay(*errs, micro - 1, 1)
        for m in range(micro):
            relay(*errs, m, 2)

    pl.when(is_last)(relay_acts)
    for m in range(micro):
        relay(*acts, m, chips - 1)

    def nearby(index):
        low = z + (index % 2) * (1 - 2 * (z % 2))
        return low + (index // 2) * (2 - 4 * ((low // 2) % 2))

    start = width * z
    mlp_weight_grads(k, z, start, True)
    chain(1, 0)
    chain(2, 0)
    mlp_weight_grads(k, nearby(1), start, False)
    chain(1, 1)
    chain(2, 1)
    for m in range(micro):
        relay(*errs, m, chips - 1)
    mlp_weight_grads(k, nearby(2), start, False)
    mlp_weight_grads(k, nearby(3), start, False)

    per_core = hidden // peers
    k.dnx[...] = k.pool[pl.ds(pl.multiple_of(width + per_core * (1 - core), per_core), per_core), :].astype(BF16)
    down_pair = to_peer(k.dnx, k.dnrx, k.dnsem.at[0], k.dnsem.at[1], sibling)
    down_pair.start()
    for chip in range(chips):
        for parity in range(2):
            k.upx[chip, parity] = k.pool[
                share * (2 * chip + parity) : share * (2 * chip + parity + 1), :
            ].astype(BF16)
    up_pair = to_peer(k.upx.at[:, 1 - core], k.uprx, k.upsem.at[0], k.upsem.at[1], sibling)
    up_pair.start()
    up_pair.wait()

    def spread(chip):
        return to_peer(
            k.upx.at[chip, core], k.uax.at[z], k.uasend.at[chip], k.uarecv.at[z], 2 * chip + core
        )

    def gathered(chip):
        return to_peer(
            k.upx.at[chip, core], k.uax.at[chip], k.uasend.at[chip], k.uarecv.at[chip], 2 * chip + core
        )

    finals = []
    for chip in range(chips):
        at = part_rows(chip, core)
        total = k.pool[at, :] + k.uprx[chip].astype(F32)
        k.pool[at, :] = total
        k.upx[chip, core] = total.astype(BF16)

        @pl.when(z != chip)
        def _():
            spread(chip).start()

    down_pair.wait()
    down_at = pl.ds(pl.multiple_of(width + per_core * core, per_core), per_core)
    k.pool[down_at, :] += k.dnrx[...].astype(F32)
    final = pltpu.make_async_copy(k.pool.at[down_at], k.down_grad, k.gsem.at[0])
    final.start()
    finals.append(final)

    for part in range(2, 4):
        chain(1, part)
        chain(2, part)
    for part in range(4):
        at = part_rows(part, 1 - core)
        k.pool[at, :] = part_ref(part, z, core)[...].astype(F32)

        @pl.when(z > 0)
        def _():
            chain_copy(True, part, z).wait_recv()
            k.pool[at, :] += k.rsx[0, part, z - 1].astype(F32)

        @pl.when(z < chips - 1)
        def _():
            chain_copy(False, part, chips - 1 - z).wait_recv()
            k.pool[at, :] += k.rsx[1, part, chips - 2 - z].astype(F32)

        target = k.qkv_grad.at[:, pl.ds(part * width, width)] if part < 3 else k.out_grad
        final = pltpu.make_async_copy(k.pool.at[at], target, k.gsem.at[1 + part])
        final.start()
        finals.append(final)
    for chip in range(chips):
        at = part_rows(chip, core)

        @pl.when(z != chip)
        def _():
            gathered(chip).wait_recv()
            k.pool[at, :] = k.uax[chip].astype(F32)

        final = pltpu.make_async_copy(
            k.pool.at[at], k.up_grad.at[:, pl.ds(chip * width, width)], k.gsem.at[5 + chip]
        )
        final.start()
        finals.append(final)
    own = gvec[:, pl.ds(pl.multiple_of(me * length, 128), length)]
    for step in range(1, peers):
        vector_copy(step).wait()
        own = own + k.vrx[step]
    k.vector_grad[...] = own

    for m in range(micro):
        settle(*acts, m)
        settle(*errs, m)
    for part in range(4):
        for up in (True, False):
            for place in range(1, chips):
                @pl.when((z if up else chips - 1 - z) < place)
                def _():
                    chain_copy(up, part, place).wait_send()
    for chip in range(chips):
        @pl.when(z != chip)
        def _():
            spread(chip).wait_send()
    for final in finals:
        final.wait()
    finish_hops()


def shards(patches, lengths, qkv_weight, out_weight, up_weight, down_weight, vectors, cotangent):
    micro, _, rows, width = patches.shape
    hidden = up_weight.shape[2]
    peers = lax.axis_size("dp")
    fused = peers == 8 and hidden == peers // 2 * width
    chips = peers // 2 if fused else 1
    plan = scratch_plan(micro, rows, width, hidden, chips, peers, fused)
    anywhere = pl.BlockSpec(memory_space=pl.ANY)
    in_vmem = pl.BlockSpec(memory_space=pltpu.VMEM)
    kept = F32 if fused else BF16
    cut = peers if fused else 1
    results = pl.pallas_call(
        partial(pipeline_kernel, tuple(plan), fused),
        out_shape=(
            jax.ShapeDtypeStruct((micro, rows, width), BF16),
            jax.ShapeDtypeStruct((micro, rows, width), F32),
            jax.ShapeDtypeStruct((width // cut, 3 * width), kept),
            jax.ShapeDtypeStruct((width // cut, width), kept),
            jax.ShapeDtypeStruct((width // cut, hidden), kept),
            jax.ShapeDtypeStruct((hidden // cut, width), kept),
            jax.ShapeDtypeStruct((1, vectors.shape[1] // cut), F32),
        ),
        in_specs=[
            anywhere,
            pl.BlockSpec(memory_space=pltpu.SMEM),
            anywhere,
            anywhere,
            anywhere,
            anywhere,
            in_vmem,
            anywhere,
        ],
        out_specs=(anywhere,) * 6 + (in_vmem,),
        scratch_shapes=list(plan.values()),
        compiler_params=pltpu.CompilerParams(
            collective_id=0, has_side_effects=True, vmem_limit_bytes=62 << 20
        ),
    )(
        patches[:, 0],
        lengths,
        qkv_weight,
        out_weight,
        up_weight,
        down_weight,
        vectors,
        cotangent[:, 0],
    )
    outputs, input_grads, *grads, vector_grad = results
    if fused:
        grads = [grad[None] for grad in grads]
    else:
        grads = [
            lax.psum_scatter(grad[None], "dp", scatter_dimension=1, tiled=True).astype(F32)
            for grad in grads
        ]
        vector_grad = lax.psum_scatter(vector_grad, "dp", scatter_dimension=1, tiled=True)
    return (outputs[None, :, None], input_grads[None, :, None], *grads, vector_grad)


def solution(mesh):
    placed = (
        P(None, "dp", None, None),
        P(None, "dp"),
        P("section", None, None),
        P("section", None, None),
        P("section", None, None),
        P("section", None, None),
        P("section", None),
        P(None, "dp", None, None),
    )
    return jax.shard_map(
        shards,
        mesh=mesh,
        in_specs=placed,
        out_specs=(
            P("section", None, "dp", None, None),
            P("section", None, "dp", None, None),
            P("section", "dp", None),
            P("section", "dp", None),
            P("section", "dp", None),
            P("section", "dp", None),
            P("section", "dp"),
        ),
        check_vma=False,
    )
```

```python
from functools import partial

import jax
import jax.numpy as jnp
from jax import lax
from jax.experimental import pallas as pl
from jax.experimental.pallas import tpu as pltpu
from jax.sharding import PartitionSpec as P

HEAD_DIM = 64
EPS = 1e-06
F32 = jnp.float32
BF16 = jnp.bfloat16
MESH = pl.DeviceIdType.MESH


def nn(left, right):
    return jnp.dot(left, right, preferred_element_type=F32)


def nt(left, right):
    return lax.dot_general(left, right, (((1,), (1,)), ((), ())), preferred_element_type=F32)


def tn(left, right):
    return lax.dot_general(left, right, (((0,), (0,)), ((), ())), preferred_element_type=F32)


def normalize(hidden):
    centered = hidden - jnp.mean(hidden, axis=-1, keepdims=True)
    inverse = lax.rsqrt(jnp.mean(centered * centered, axis=-1, keepdims=True) + EPS)
    return centered * inverse, inverse


def norm_back(grad, unit, inverse):
    average = jnp.mean(grad, axis=-1, keepdims=True)
    slope = jnp.mean(grad * unit, axis=-1, keepdims=True)
    return inverse * (grad - average - unit * slope)


def gelu_pair(u):
    phi = 0.5 + 0.5 * lax.erf(u * 0.7071067811865476)
    density = jnp.exp(u * u * -0.5) * 0.3989422804014327
    return u * phi, phi + u * density


class Refs:
    def __init__(self, names, refs):
        self.__dict__.update(zip(names, refs))


INPUTS = ("patches", "lengths", "wqkv_h", "wout_h", "wup_h", "wdown_h", "vec", "cot")
RESULTS = ("outputs", "input_grads", "qkv_grad", "out_grad", "up_grad", "down_grad", "vector_grad")


def scratch_plan(micro, rows, width, hidden, chips, peers, fused):
    heads = width // HEAD_DIM
    dma = pltpu.SemaphoreType.DMA
    vm = pltpu.VMEM
    act = vm((micro, rows, width), BF16)
    blocks = vm((micro, chips, rows, width), BF16)
    plan = dict(
        wqkv=vm((width, 3 * width), BF16),
        wout=vm((width, width), BF16),
        wup=vm((width, hidden), BF16),
        wdown=vm((hidden, width), BF16),
        x=act, a1=act, n1=act, o=act, n2=act, y=act, a2=blocks, e=blocks,
        r1=vm((micro, rows, 128), F32),
        r2=vm((micro, rows, 128), F32),
        qkv=vm((micro, rows, 3 * width), BF16),
        bias=vm((1, 3 * width), F32),
        p=vm((micro, heads, rows, rows), BF16),
        wide=vm((rows, hidden), BF16),
        gp=vm((micro, rows, hidden), BF16),
        dp=vm((micro, rows, 3 * width), BF16),
        do=vm((rows, width), BF16),
        doo=vm((rows, width), BF16),
        rest=vm((rows, width), BF16),
        pool=vm((2 * width, width), F32),
        ig=vm((micro, rows, width), F32),
        lens=pltpu.SMEM((micro,), jnp.int32),
        lsem=dma((1,)),
        wsem=dma((4,)),
        psem=dma((micro,)),
        csem=dma((micro,)),
        xsend=dma((micro,)),
        xrecv=dma((micro,)),
        esend=dma((micro,)),
        erecv=dma((micro,)),
        osem=dma((micro,)),
        isem=dma((micro,)),
        gsem=dma((3 * chips,)),
    )
    if fused:
        share = width // peers
        plan.update(
            gvec=vm((1, 8 * width + hidden), F32),
            asend=dma((2, micro, chips)),
            arecv=dma((micro, chips)),
            bsend=dma((2, micro, chips)),
            brecv=dma((micro, chips)),
            prx=vm((4, chips, share, width), BF16),
            pxsend=dma((4, chips)),
            pxrecv=dma((4, chips)),
            rsx=vm((2, 4, chips - 1, share, width), BF16),
            rsend=dma((2, 4, chips)),
            rrecv=dma((2, 4, chips)),
            vrx=vm((peers, 1, (8 * width + hidden) // peers), F32),
            vsend=dma((peers,)),
            vrecv=dma((peers,)),
            upx=vm((chips, 2, share, width), BF16),
            uprx=vm((chips, share, width), BF16),
            upsem=dma((2,)),
            dnx=vm((hidden // peers, width), BF16),
            dnrx=vm((hidden // peers, width), BF16),
            dnsem=dma((2,)),
            uax=vm((chips, share, width), BF16),
            uasend=dma((chips,)),
            uarecv=dma((chips,)),
            turn=pltpu.SemaphoreType.REGULAR,
        )
    return plan


def pair_masks():
    lane = lax.broadcasted_iota(jnp.int32, (1, 128), 1)
    return (lane < HEAD_DIM).astype(BF16), (lane >= HEAD_DIM).astype(BF16), lane < HEAD_DIM


def pool_rows(k, block, m=0):
    rows = k.x.shape[1]
    return pl.ds(pl.multiple_of((block + m) * rows, rows), rows)


RL, OF, MID = 0, 2, 4


def forward_attention(k, m, z, key_bias):
    rows, width = k.x.shape[1:]
    vec = k.vec
    unit, inverse = normalize(k.x[m].astype(F32))
    k.n1[m] = unit.astype(BF16)
    k.r1[m] = jnp.broadcast_to(inverse, (rows, 128))
    k.a1[m] = (unit * (1.0 + vec[:, :width]) + vec[:, width : 2 * width]).astype(BF16)
    normed = k.a1[m]
    for c in range(0, 3 * width, 256):
        k.qkv[m, :, c : c + 256] = (nn(normed, k.wqkv[:, c : c + 256]) + k.bias[:, c : c + 256]).astype(BF16)
    low, high, first = pair_masks()
    ones = jnp.ones((rows, 128), BF16)
    for c in range(0, width, 128):
        queries = k.qkv[m, :, c : c + 128]
        keys = k.qkv[m, :, width + c : width + c + 128]
        values = jnp.concatenate([k.qkv[m, :, 2 * width + c : 2 * width + c + 128], ones], axis=1)
        sums = []
        for half, mask in enumerate((low, high)):
            scores = nt(queries * (mask * jnp.asarray(HEAD_DIM**-0.5, BF16)), keys) + key_bias
            top = jnp.max(scores, axis=-1, keepdims=True)
            raised = jnp.exp(scores - top).astype(BF16)
            k.p[m, c // HEAD_DIM + half] = raised
            sums.append(nn(raised, values))
        inverse_sum = 1.0 / jnp.where(first, sums[0][:, 128:], sums[1][:, 128:])
        k.pool[pool_rows(k, RL, m), c : c + 128] = inverse_sum
        joined = jnp.where(first, sums[0][:, :128], sums[1][:, :128]) * inverse_sum
        k.pool[pool_rows(k, OF, m), c : c + 128] = joined
        k.o[m, :, c : c + 128] = joined.astype(BF16)
    attended = k.o[m]
    mid = pool_rows(k, MID)
    for c in range(0, width, 256):
        k.pool[mid, c : c + 256] = k.x[m, :, c : c + 256].astype(F32) + (
            nn(attended, k.wout[:, c : c + 256]) + vec[:, 4 * width + c : 4 * width + c + 256]
        )
    unit, inverse = normalize(k.pool[mid, :])
    k.n2[m] = unit.astype(BF16)
    k.r2[m] = jnp.broadcast_to(inverse, (rows, 128))
    k.a2[m, z] = (unit * (1.0 + vec[:, 5 * width : 6 * width]) + vec[:, 6 * width : 7 * width]).astype(BF16)


def forward_mlp(k, m, z):
    width = k.x.shape[2]
    vec = k.vec
    normed = k.a2[m, z]
    for c in range(0, k.wup.shape[1], 256):
        u = nn(normed, k.wup[:, c : c + 256]) + vec[:, 8 * width + c : 8 * width + c + 256]
        value, slope = gelu_pair(u)
        k.wide[:, c : c + 256] = value.astype(BF16)
        k.gp[m, :, c : c + 256] = slope.astype(BF16)
    added = nn(k.wide[...], k.wdown[...]) + vec[:, 7 * width : 8 * width]
    k.y[m] = (k.pool[pool_rows(k, MID), :] + added).astype(BF16)


def add_sums(ref, at, value):
    ref[:, at : at + value.shape[1]] += jnp.sum(value, axis=0, keepdims=True)


def backward_mlp(k, gvec, m, z):
    width = k.x.shape[2]
    vec = k.vec
    grad = k.e[m, z]
    add_sums(gvec, 7 * width, grad.astype(F32))
    for c in range(0, k.wup.shape[1], 256):
        grad_up = (
            nt(grad, k.wdown[c : c + 256, :]) * k.gp[m, :, c : c + 256].astype(F32)
        ).astype(BF16)
        k.wide[:, c : c + 256] = grad_up
        add_sums(gvec, 8 * width + c, grad_up.astype(F32))
    grad_two = nt(k.wide[...], k.wup[...])
    unit = k.n2[m].astype(F32)
    add_sums(gvec, 5 * width, grad_two * unit)
    add_sums(gvec, 6 * width, grad_two)
    grad_mid = k.e[m, z].astype(F32) + norm_back(
        grad_two * (1.0 + vec[:, 5 * width : 6 * width]), unit, k.r2[m, :, :1]
    )
    k.pool[pool_rows(k, MID), :] = grad_mid
    branch = grad_mid.astype(BF16)
    k.x[m] = branch
    add_sums(gvec, 4 * width, branch.astype(F32))


def backward_attention(k, gvec, m):
    rows, width = k.x.shape[1:]
    vec = k.vec
    k.do[...] = (nt(k.x[m], k.wout[...]) * k.pool[pool_rows(k, RL, m), :]).astype(BF16)
    product = k.do[...].astype(F32) * k.pool[pool_rows(k, OF, m), :]
    k.doo[...] = product.astype(BF16)
    k.rest[...] = (product - k.doo[...].astype(F32)).astype(BF16)
    low, high, first = pair_masks()
    minus = jnp.full((rows, 128), -1.0, BF16)
    scale = HEAD_DIM**-0.5
    for c in range(0, width, 128):
        queries = k.qkv[m, :, c : c + 128]
        keys = k.qkv[m, :, width + c : width + c + 128]
        values = jnp.concatenate([k.qkv[m, :, 2 * width + c : 2 * width + c + 128], minus], axis=1)
        grads = k.do[:, c : c + 128]
        inner = k.doo[:, c : c + 128]
        rest = pltpu.roll(k.rest[:, c : c + 128].astype(F32), HEAD_DIM, 1).astype(BF16)
        inners = (jnp.where(first, inner, rest), jnp.where(first, rest, inner))
        total_q = total_k = total_v = 0.0
        for half, mask in enumerate((low, high)):
            raised = k.p[m, c // HEAD_DIM + half]
            left = jnp.concatenate([grads * mask, inners[half]], axis=1)
            grad_scores = (raised.astype(F32) * nt(left, values)).astype(BF16)
            total_v = total_v + tn(raised, grads * mask)
            total_q = total_q + nn(grad_scores, keys * mask)
            total_k = total_k + tn(grad_scores, queries * mask)
        grad_q = (total_q * scale).astype(BF16)
        grad_v = total_v.astype(BF16)
        k.dp[m, :, c : c + 128] = grad_q
        k.dp[m, :, width + c : width + c + 128] = (total_k * scale).astype(BF16)
        k.dp[m, :, 2 * width + c : 2 * width + c + 128] = grad_v
        add_sums(gvec, 2 * width + c, grad_q.astype(F32))
        add_sums(gvec, 3 * width + c, grad_v.astype(F32))
    grad_one = nt(k.dp[m], k.wqkv[...])
    unit = k.n1[m].astype(F32)
    add_sums(gvec, 0, grad_one * unit)
    add_sums(gvec, width, grad_one)
    grad_in = k.pool[pool_rows(k, MID), :] + norm_back(
        grad_one * (1.0 + vec[:, :width]), unit, k.r1[m, :, :1]
    )
    k.ig[m] = grad_in
    k.y[m] = grad_in.astype(BF16)


def attention_weight_grads(k, after_chunk):
    micro, rows, width = k.x.shape
    both = micro * rows
    normed = k.a1[...].reshape(both, width)
    for part in range(3):
        grads = k.dp[:, :, part * width : (part + 1) * width].reshape(both, width)
        k.wqkv[:, part * width : (part + 1) * width] = tn(normed, grads).astype(BF16)
        after_chunk(part)
    k.wout[...] = tn(k.o[...].reshape(both, width), k.x[...].reshape(both, width)).astype(BF16)
    after_chunk(3)


def mlp_weight_grads(k, origin, start, fresh):
    micro, rows, width = k.x.shape
    both = micro * rows
    normed = k.a2[:, origin].reshape(both, width)
    grad = k.e[:, origin].reshape(both, width)
    for c in range(0, width, 256):
        at = pl.ds(pl.multiple_of(start + c, 256), 256)
        u = nn(normed, k.wup[:, at]) + k.vec[:, pl.ds(pl.multiple_of(8 * width + start + c, 256), 256)]
        value, slope = gelu_pair(u)
        grad_up = (nt(grad, k.wdown[at, :]) * slope).astype(BF16)
        up = tn(normed, grad_up)
        down = tn(value.astype(BF16), grad)
        if fresh:
            k.pool[:width, c : c + 256] = up
            k.pool[width + c : width + c + 256, :] = down
        else:
            k.pool[:width, c : c + 256] += up
            k.pool[width + c : width + c + 256, :] += down


def pipeline_kernel(scratch_names, fused, *refs):
    k = Refs(INPUTS + RESULTS + scratch_names, refs)
    sec = lax.axis_index("section")
    count = lax.axis_size("section")
    peers = lax.axis_size("dp")
    me = lax.axis_index("dp")
    micro, rows, width = k.x.shape
    hidden = k.wup.shape[1]
    chips = k.e.shape[1]
    z, core = (me // 2, me % 2) if fused else (0, 0)
    gvec = k.gvec if fused else k.vector_grad
    share = width // peers
    is_first = sec == 0
    is_last = sec == count - 1
    not_last = sec < count - 1
    after = jnp.minimum(sec + 1, count - 1)
    before = jnp.maximum(sec - 1, 0)

    barrier = pltpu.get_barrier_semaphore()

    @pl.when(sec > 0)
    def _():
        pl.semaphore_signal(barrier, inc=1, device_id={"section": before}, device_id_type=MESH)

    @pl.when(not_last)
    def _():
        pl.semaphore_signal(barrier, inc=1, device_id={"section": after}, device_id_type=MESH)

    if fused:
        for step in range(1, peers):
            pl.semaphore_signal(
                barrier, inc=1, device_id={"dp": (me + step) % peers}, device_id_type=MESH
            )

    def patch_copy(m):
        return pltpu.make_async_copy(k.patches.at[m], k.x.at[m], k.psem.at[m])

    def cot_copy(m):
        return pltpu.make_async_copy(k.cot.at[m], k.e.at[m, z], k.csem.at[m])

    loads = [
        pltpu.make_async_copy(src.at[0], dst, k.wsem.at[i])
        for i, (src, dst) in enumerate(
            ((k.wqkv_h, k.wqkv), (k.wout_h, k.wout), (k.wup_h, k.wup), (k.wdown_h, k.wdown))
        )
    ]

    @pl.when(is_first)
    def _():
        for m in range(micro):
            patch_copy(m).start()

    lens_copy = pltpu.make_async_copy(k.lengths, k.lens, k.lsem.at[0])
    lens_copy.start()
    loads[0].start()
    loads[1].start()

    @pl.when(is_last)
    def _():
        for m in range(micro):
            cot_copy(m).start()

    k.bias[:, :width] = k.vec[:, 2 * width : 3 * width]
    k.bias[:, width : 2 * width] = jnp.zeros((1, width), F32)
    k.bias[:, 2 * width :] = k.vec[:, 3 * width : 4 * width]
    gvec[...] = jnp.zeros_like(gvec)
    lens_copy.wait()
    loads[0].wait()
    loads[1].wait()
    loads[2].start()
    loads[3].start()

    def y_send(m):
        return pltpu.make_async_remote_copy(
            src_ref=k.y.at[m], dst_ref=k.x.at[m], send_sem=k.xsend.at[m], recv_sem=k.xrecv.at[m],
            device_id={"section": after}, device_id_type=MESH,
        )

    def e_send(m):
        return pltpu.make_async_remote_copy(
            src_ref=k.y.at[m], dst_ref=k.e.at[m, z], send_sem=k.esend.at[m], recv_sem=k.erecv.at[m],
            device_id={"section": before}, device_id_type=MESH,
        )

    def out_copy(m):
        return pltpu.make_async_copy(k.y.at[m], k.outputs.at[m], k.osem.at[m])

    def in_copy(m):
        return pltpu.make_async_copy(k.ig.at[m], k.input_grads.at[m], k.isem.at[m])

    def to_peer(src, dst, send, recv, device):
        return pltpu.make_async_remote_copy(
            src_ref=src, dst_ref=dst, send_sem=send, recv_sem=recv,
            device_id={"dp": device}, device_id_type=MESH,
        )

    def pass_on(ref, sends, recvs, m, origin, up):
        return to_peer(
            ref.at[m, origin], ref.at[m, origin], sends.at[0 if up else 1, m, origin],
            recvs.at[m, origin], me + 2 if up else me - 2,
        )

    def share_own(ref, sends, recvs, m):
        @pl.when(z < chips - 1)
        def _():
            pass_on(ref, sends, recvs, m, z, True).start()

        @pl.when(z > 0)
        def _():
            pass_on(ref, sends, recvs, m, z, False).start()

    def relay(ref, sends, recvs, m, distance):
        @pl.when(z >= distance)
        def _():
            pass_on(ref, sends, recvs, m, z - distance, True).wait_recv()

            @pl.when(z < chips - 1)
            def _():
                pass_on(ref, sends, recvs, m, z - distance, True).start()

        @pl.when(z + distance < chips)
        def _():
            pass_on(ref, sends, recvs, m, z + distance, False).wait_recv()

            @pl.when(z > 0)
            def _():
                pass_on(ref, sends, recvs, m, z + distance, False).start()

    def settle(ref, sends, recvs, m):
        for distance in range(chips):
            @pl.when((z >= distance) & (z < chips - 1))
            def _():
                pass_on(ref, sends, recvs, m, z - distance, True).wait_send()

            @pl.when((z + distance < chips) & (z > 0))
            def _():
                pass_on(ref, sends, recvs, m, z + distance, False).wait_send()

    if fused:
        acts = (k.a2, k.asend, k.arecv)
        errs = (k.e, k.bsend, k.brecv)
    arrivals = (sec > 0).astype(jnp.int32) + not_last.astype(jnp.int32)
    pl.semaphore_wait(barrier, arrivals + (peers - 1 if fused else 0))

    @pl.when(is_last)
    def _():
        for m in range(micro):
            cot_copy(m).wait()
            valid = lax.broadcasted_iota(jnp.int32, (rows, width), 0) < k.lens[m]
            k.e[m, z] = jnp.where(valid, k.e[m, z].astype(F32), 0.0).astype(BF16)
            if fused:
                share_own(*errs, m)
        if fused:
            for distance in range(1, chips - 1):
                for m in range(micro):
                    relay(*errs, m, distance)

    waits_turn = is_first & (core == 1) & not_last

    def forward_step(m):
        @pl.when(is_first)
        def _():
            patch_copy(m).wait()

        @pl.when(sec > 0)
        def _():
            y_send(m).wait_recv()

        key_bias = jnp.where(
            lax.broadcasted_iota(jnp.int32, (1, rows), 1) < k.lens[m], 0.0, -1e30
        )
        forward_attention(k, m, z, key_bias)
        if fused:
            share_own(*acts, m)

            @pl.when(waits_turn & (m > 0))
            def _():
                y_send(m - 1).start()

        @pl.when(m == 0)
        def _():
            loads[2].wait()
            loads[3].wait()

        forward_mlp(k, m, z)

        @pl.when(not_last & jnp.logical_not(waits_turn))
        def _():
            y_send(m).start()

        out_copy(m).start()

    def relay_acts(*distances):
        for distance in distances:
            for m in range(micro):
                relay(*acts, m, distance)

    def backward_step(m):
        out_copy(m).wait()

        @pl.when(not_last)
        def _():
            e_send(m).wait_recv()
            if fused:
                share_own(*errs, m)

        backward_mlp(k, gvec, m, z)
        if fused:
            @pl.when(is_first & not_last & (m == micro - 1))
            def _():
                for early in range(micro - 1):
                    relay(*errs, early, 2)

        backward_attention(k, gvec, m)

        @pl.when(sec > 0)
        def _():
            e_send(m).start()

        in_copy(m).start()
        if fused:
            @pl.when(is_first & not_last & (m < micro - 1))
            def _():
                relay(*errs, m, 1)

    def turn_round():
        if fused:
            @pl.when(is_first & (core == 0) & not_last)
            def _():
                y_send(micro - 1).wait_send()
                pl.semaphore_signal(k.turn, inc=1, device_id={"dp": me + 1}, device_id_type=MESH)

            @pl.when(waits_turn)
            def _():
                pl.semaphore_wait(k.turn, 1)
                y_send(micro - 1).start()
        for m in range(micro):
            waited = is_first & (core == 0) if fused and m == micro - 1 else False

            @pl.when(jnp.logical_not(waited))
            def _():
                y_send(m).wait_send()

        if fused:
            relay_acts(1)
            pl.when(sec < count - 2)(lambda: relay_acts(*range(2, chips - 1)))

    def step(index, carry):
        forward = jnp.where(is_last, index % 2 == 0, index < micro)
        m = jnp.where(is_last, index // 2, index % micro)
        pl.when(forward)(lambda: forward_step(m))
        pl.when(not_last & (index == micro))(turn_round)
        pl.when(jnp.logical_not(forward))(lambda: backward_step(m))
        return carry

    lax.fori_loop(0, 2 * micro, step, 0)

    def finish_hops():
        for m in range(micro):
            in_copy(m).wait()

            @pl.when(sec > 0)
            def _():
                e_send(m).wait_send()

    if not fused:
        attention_weight_grads(k, lambda part: None)
        for c in range(0, hidden, width):
            mlp_weight_grads(k, 0, c, True)
            k.wup[:, c : c + width] = k.pool[:width, :].astype(BF16)
            k.wdown[c : c + width, :] = k.pool[width:, :].astype(BF16)
        copies = [
            pltpu.make_async_copy(src, dst, k.wsem.at[i])
            for i, (src, dst) in enumerate(
                ((k.wqkv, k.qkv_grad), (k.wout, k.out_grad), (k.wup, k.up_grad), (k.wdown, k.down_grad))
            )
        ]
        for copy in copies:
            copy.start()
        for copy in copies:
            copy.wait()
        finish_hops()
        return

    sibling = me + 1 - 2 * core

    def part_rows(chip, parity):
        return pl.ds(pl.multiple_of(share * (2 * chip + parity), share), share)

    def part_ref(part, chip, parity):
        if part < 3:
            return k.wqkv.at[part_rows(chip, parity), pl.ds(part * width, width)]
        return k.wout.at[part_rows(chip, parity), :]

    def pair_copy(part, chip):
        return to_peer(
            part_ref(part, chip, 1 - core), k.prx.at[part, chip],
            k.pxsend.at[part, chip], k.pxrecv.at[part, chip], sibling,
        )

    def send_pair(part):
        for chip in range(chips):
            pair_copy(part, chip).start()

    attention_weight_grads(k, send_pair)

    length = gvec.shape[1] // peers

    def vector_copy(step):
        device = (me + step) % peers
        return to_peer(
            gvec.at[:, pl.ds(pl.multiple_of(device * length, 128), length)], k.vrx.at[step],
            k.vsend.at[step], k.vrecv.at[step], device,
        )

    for step in range(1, peers):
        vector_copy(step).start()

    def chain_copy(up, part, place):
        chip = place if up else chips - 1 - place
        lane = 0 if up else 1
        return to_peer(
            part_ref(part, chip, core), k.rsx.at[lane, part, place - 1],
            k.rsend.at[lane, part, place], k.rrecv.at[lane, part, place],
            me + 2 if up else me - 2,
        )

    def chain(stage, part):
        for up in (True, False):
            @pl.when((z if up else chips - 1 - z) == stage)
            def _():
                for place in range(chips - 1, stage, -1):
                    if stage > 0:
                        chain_copy(up, part, place).wait_recv()
                        chip = place if up else chips - 1 - place
                        target = part_ref(part, chip, core)
                        target[...] = (
                            target[...].astype(F32)
                            + k.rsx[0 if up else 1, part, place - 1].astype(F32)
                        ).astype(BF16)
                    chain_copy(up, part, place).start()

    for part in range(4):
        for chip in range(chips):
            pair_copy(part, chip).wait()
            target = part_ref(part, chip, core)
            target[...] = (target[...].astype(F32) + k.prx[part, chip].astype(F32)).astype(BF16)
        chain(0, part)

    def nearby(index):
        low = z + (index % 2) * (1 - 2 * (z % 2))
        return low + (index // 2) * (2 - 4 * ((low // 2) % 2))

    start = width * z

    @pl.when(not_last & (sec > 0))
    def _():
        for early in range(micro - 1):
            relay(*errs, early, 1)

    @pl.when(not_last)
    def _():
        relay(*errs, micro - 1, 1)

    @pl.when(not_last & (sec > 0))
    def _():
        for early in range(micro - 1):
            relay(*errs, early, 2)

    pl.when(is_last)(lambda: relay_acts(1))
    pl.when(sec >= count - 2)(lambda: relay_acts(*range(2, chips - 1)))
    mlp_weight_grads(k, z, start, True)
    chain(1, 0)

    @pl.when(not_last)
    def _():
        relay(*errs, micro - 1, 2)

    mlp_weight_grads(k, nearby(1), start, False)
    chain(1, 1)
    mlp_weight_grads(k, nearby(2), start, False)
    chain(1, 2)
    for m in range(micro):
        relay(*acts, m, chips - 1)
        relay(*errs, m, chips - 1)
    mlp_weight_grads(k, nearby(3), start, False)

    per_core = hidden // peers
    k.dnx[...] = k.pool[pl.ds(pl.multiple_of(width + per_core * (1 - core), per_core), per_core), :].astype(BF16)
    down_pair = to_peer(k.dnx, k.dnrx, k.dnsem.at[0], k.dnsem.at[1], sibling)
    down_pair.start()
    for chip in range(chips):
        for parity in range(2):
            k.upx[chip, parity] = k.pool[
                share * (2 * chip + parity) : share * (2 * chip + parity + 1), :
            ].astype(BF16)
    up_pair = to_peer(k.upx.at[:, 1 - core], k.uprx, k.upsem.at[0], k.upsem.at[1], sibling)
    up_pair.start()
    up_pair.wait()

    def spread(chip):
        return to_peer(
            k.upx.at[chip, core], k.uax.at[z], k.uasend.at[chip], k.uarecv.at[z], 2 * chip + core
        )

    def gathered(chip):
        return to_peer(
            k.upx.at[chip, core], k.uax.at[chip], k.uasend.at[chip], k.uarecv.at[chip], 2 * chip + core
        )

    finals = []
    for chip in range(chips):
        at = part_rows(chip, core)
        total = k.pool[at, :] + k.uprx[chip].astype(F32)
        k.pool[at, :] = total
        k.upx[chip, core] = total.astype(BF16)

        @pl.when(z != chip)
        def _():
            spread(chip).start()

    down_pair.wait()
    down_at = pl.ds(pl.multiple_of(width + per_core * core, per_core), per_core)
    k.pool[down_at, :] += k.dnrx[...].astype(F32)
    final = pltpu.make_async_copy(k.pool.at[down_at], k.down_grad, k.gsem.at[0])
    final.start()
    finals.append(final)

    for part in range(3):
        chain(2, part)
    chain(1, 3)
    chain(2, 3)
    for part in range(4):
        at = part_rows(part, 1 - core)
        k.pool[at, :] = part_ref(part, z, core)[...].astype(F32)

        @pl.when(z > 0)
        def _():
            chain_copy(True, part, z).wait_recv()
            k.pool[at, :] += k.rsx[0, part, z - 1].astype(F32)

        @pl.when(z < chips - 1)
        def _():
            chain_copy(False, part, chips - 1 - z).wait_recv()
            k.pool[at, :] += k.rsx[1, part, chips - 2 - z].astype(F32)

        target = k.qkv_grad.at[:, pl.ds(part * width, width)] if part < 3 else k.out_grad
        final = pltpu.make_async_copy(k.pool.at[at], target, k.gsem.at[1 + part])
        final.start()
        finals.append(final)
    for chip in range(chips):
        at = part_rows(chip, core)

        @pl.when(z != chip)
        def _():
            gathered(chip).wait_recv()
            k.pool[at, :] = k.uax[chip].astype(F32)

        final = pltpu.make_async_copy(
            k.pool.at[at], k.up_grad.at[:, pl.ds(chip * width, width)], k.gsem.at[5 + chip]
        )
        final.start()
        finals.append(final)
    own = gvec[:, pl.ds(pl.multiple_of(me * length, 128), length)]
    for step in range(1, peers):
        vector_copy(step).wait()
        own = own + k.vrx[step]
    k.vector_grad[...] = own

    for m in range(micro):
        settle(*acts, m)
        settle(*errs, m)
    for part in range(4):
        for up in (True, False):
            for place in range(1, chips):
                @pl.when((z if up else chips - 1 - z) < place)
                def _():
                    chain_copy(up, part, place).wait_send()
    for chip in range(chips):
        @pl.when(z != chip)
        def _():
            spread(chip).wait_send()
    for final in finals:
        final.wait()
    finish_hops()


def deliver_kernel(count, *refs):
    sources, targets, held = refs[:count], refs[count : 2 * count], refs[2 * count : 3 * count]
    sems = refs[-1]
    fetches = [
        pltpu.make_async_copy(sources[i], held[i], sems.at[0, i]) for i in range(count)
    ]
    stores = [
        pltpu.make_async_copy(held[i], targets[i], sems.at[1, i]) for i in range(count)
    ]
    for fetch in fetches:
        fetch.start()
    for fetch, store in zip(fetches, stores):
        fetch.wait()
        store.start()
    for store in stores:
        store.wait()


def deliver(arrays):
    anywhere = pl.BlockSpec(memory_space=pl.ANY)
    count = len(arrays)
    return pl.pallas_call(
        partial(deliver_kernel, count),
        out_shape=tuple(jax.ShapeDtypeStruct(a.shape, a.dtype) for a in arrays),
        in_specs=[anywhere] * count,
        out_specs=(anywhere,) * count,
        scratch_shapes=[pltpu.VMEM(a.shape, a.dtype) for a in arrays]
        + [pltpu.SemaphoreType.DMA((2, count))],
        compiler_params=pltpu.CompilerParams(vmem_limit_bytes=62 << 20),
    )(*arrays)


def shards(patches, lengths, qkv_weight, out_weight, up_weight, down_weight, vectors, cotangent):
    micro, _, rows, width = patches.shape
    hidden = up_weight.shape[2]
    peers = lax.axis_size("dp")
    fused = peers == 8 and hidden == peers // 2 * width
    chips = peers // 2 if fused else 1
    plan = scratch_plan(micro, rows, width, hidden, chips, peers, fused)
    anywhere = pl.BlockSpec(memory_space=pl.ANY)
    in_vmem = pl.BlockSpec(memory_space=pltpu.VMEM)
    kept = F32 if fused else BF16
    cut = peers if fused else 1
    results = pl.pallas_call(
        partial(pipeline_kernel, tuple(plan), fused),
        out_shape=(
            jax.ShapeDtypeStruct((micro, rows, width), BF16),
            jax.ShapeDtypeStruct((micro, rows, width), F32),
            jax.ShapeDtypeStruct((width // cut, 3 * width), kept),
            jax.ShapeDtypeStruct((width // cut, width), kept),
            jax.ShapeDtypeStruct((width // cut, hidden), kept),
            jax.ShapeDtypeStruct((hidden // cut, width), kept),
            jax.ShapeDtypeStruct((1, vectors.shape[1] // cut), F32),
        ),
        in_specs=[
            anywhere,
            anywhere,
            anywhere,
            anywhere,
            anywhere,
            anywhere,
            in_vmem,
            anywhere,
        ],
        out_specs=(anywhere,) * 6 + (in_vmem,),
        scratch_shapes=list(plan.values()),
        compiler_params=pltpu.CompilerParams(
            collective_id=0, has_side_effects=True, vmem_limit_bytes=62 << 20
        ),
    )(
        patches[:, 0],
        lengths[:, 0],
        qkv_weight,
        out_weight,
        up_weight,
        down_weight,
        vectors,
        cotangent[:, 0],
    )
    if fused:
        results = deliver(results)
    outputs, input_grads, *grads, vector_grad = results
    if fused:
        grads = [grad[None] for grad in grads]
    else:
        grads = [
            lax.psum_scatter(grad[None], "dp", scatter_dimension=1, tiled=True).astype(F32)
            for grad in grads
        ]
        vector_grad = lax.psum_scatter(vector_grad, "dp", scatter_dimension=1, tiled=True)
    return (outputs[None, :, None], input_grads[None, :, None], *grads, vector_grad)


def solution(mesh):
    placed = (
        P(None, "dp", None, None),
        P(None, "dp"),
        P("section", None, None),
        P("section", None, None),
        P("section", None, None),
        P("section", None, None),
        P("section", None),
        P(None, "dp", None, None),
    )
    return jax.shard_map(
        shards,
        mesh=mesh,
        in_specs=placed,
        out_specs=(
            P("section", None, "dp", None, None),
            P("section", None, "dp", None, None),
            P("section", "dp", None),
            P("section", "dp", None),
            P("section", "dp", None),
            P("section", "dp", None),
            P("section", "dp"),
        ),
        check_vma=False,
    )
```

```python
from functools import partial

import jax
import jax.numpy as jnp
from jax import lax
from jax.experimental import pallas as pl
from jax.experimental.pallas import tpu as pltpu
from jax.sharding import PartitionSpec as P

HEAD_DIM = 64
EPS = 1e-06
F32 = jnp.float32
BF16 = jnp.bfloat16
MESH = pl.DeviceIdType.MESH


def nn(left, right):
    return jnp.dot(left, right, preferred_element_type=F32)


def nt(left, right):
    return lax.dot_general(left, right, (((1,), (1,)), ((), ())), preferred_element_type=F32)


def tn(left, right):
    return lax.dot_general(left, right, (((0,), (0,)), ((), ())), preferred_element_type=F32)


def normalize(hidden):
    centered = hidden - jnp.mean(hidden, axis=-1, keepdims=True)
    inverse = lax.rsqrt(jnp.mean(centered * centered, axis=-1, keepdims=True) + EPS)
    return centered * inverse, inverse


def norm_back(grad, unit, inverse):
    average = jnp.mean(grad, axis=-1, keepdims=True)
    slope = jnp.mean(grad * unit, axis=-1, keepdims=True)
    return inverse * (grad - average - unit * slope)


def gelu_pair(u):
    phi = 0.5 + 0.5 * lax.erf(u * 0.7071067811865476)
    density = jnp.exp(u * u * -0.5) * 0.3989422804014327
    return u * phi, phi + u * density


class Refs:
    def __init__(self, names, refs):
        self.__dict__.update(zip(names, refs))


INPUTS = ("patches", "lengths", "wqkv_h", "wout_h", "wup_h", "wdown_h", "vec", "cot")
RESULTS = ("outputs", "input_grads", "qkv_grad", "out_grad", "up_grad", "down_grad", "vector_grad")


def scratch_plan(micro, rows, width, hidden, chips, peers, fused):
    heads = width // HEAD_DIM
    dma = pltpu.SemaphoreType.DMA
    vm = pltpu.VMEM
    act = vm((micro, rows, width), BF16)
    blocks = vm((micro, chips, rows, width), BF16)
    plan = dict(
        wqkv=vm((width, 3 * width), BF16),
        wout=vm((width, width), BF16),
        wup=vm((width, hidden), BF16),
        wdown=vm((hidden, width), BF16),
        x=act, a1=act, n1=act, o=act, n2=act, y=act, a2=blocks, e=blocks,
        r1=vm((micro, rows, 128), F32),
        r2=vm((micro, rows, 128), F32),
        qkv=vm((micro, rows, 3 * width), BF16),
        bias=vm((1, 3 * width), F32),
        p=vm((micro, heads, rows, rows), BF16),
        wide=vm((rows, hidden), BF16),
        gp=vm((micro, rows, hidden), BF16),
        du=vm((micro, rows, hidden), BF16),
        dp=vm((micro, rows, 3 * width), BF16),
        do=vm((rows, width), BF16),
        doo=vm((rows, width), BF16),
        rest=vm((rows, width), BF16),
        pool=vm((chips * UP_ROWS + width, width) if fused else (2 * width, width), F32),
        ig=vm((micro, rows, width), F32),
        lens=pltpu.SMEM((micro,), jnp.int32),
        lsem=dma((1,)),
        wsem=dma((4,)),
        psem=dma((micro,)),
        csem=dma((micro,)),
        xsend=dma((micro,)),
        xrecv=dma((micro,)),
        esend=dma((micro,)),
        erecv=dma((micro,)),
        osem=dma((micro,)),
        isem=dma((micro,)),
        gsem=dma((3 * chips,)),
    )
    if fused:
        share = width // peers
        plan.update(
            gvec=vm((1, 8 * width + hidden), F32),
            asend=dma((2, micro, chips)),
            arecv=dma((micro, chips)),
            bsend=dma((2, micro, chips)),
            brecv=dma((micro, chips)),
            prx=vm((4, chips, share, width), BF16),
            pxsend=dma((4, chips)),
            pxrecv=dma((4, chips)),
            rsx=vm((2, 4, chips - 1, share, width), BF16),
            rsend=dma((2, 4, chips)),
            rrecv=dma((2, 4, chips)),
            vrx=vm((peers, 1, (8 * width + hidden) // peers), F32),
            vsend=dma((peers,)),
            vrecv=dma((peers,)),
            upx=vm((chips, share, width), BF16),
            uprx=vm((chips, share, width), BF16),
            upsem=dma((2,)),
            dnx=vm((hidden // peers, width), BF16),
            dnrx=vm((hidden // peers, width), BF16),
            dnsem=dma((2,)),
            turn=pltpu.SemaphoreType.REGULAR,
        )
    return plan


def pair_masks():
    lane = lax.broadcasted_iota(jnp.int32, (1, 128), 1)
    return (lane < HEAD_DIM).astype(BF16), (lane >= HEAD_DIM).astype(BF16), lane < HEAD_DIM


def pool_rows(k, block, m=0):
    rows = k.x.shape[1]
    return pl.ds(pl.multiple_of((block + m) * rows, rows), rows)


RL, OF, MID = 0, 2, 4
UP_ROWS = 256


def forward_attention(k, m, z, key_bias):
    rows, width = k.x.shape[1:]
    vec = k.vec
    unit, inverse = normalize(k.x[m].astype(F32))
    k.n1[m] = unit.astype(BF16)
    k.r1[m] = jnp.broadcast_to(inverse, (rows, 128))
    k.a1[m] = (unit * (1.0 + vec[:, :width]) + vec[:, width : 2 * width]).astype(BF16)
    normed = k.a1[m]
    for c in range(0, 3 * width, 256):
        k.qkv[m, :, c : c + 256] = (nn(normed, k.wqkv[:, c : c + 256]) + k.bias[:, c : c + 256]).astype(BF16)
    low, high, first = pair_masks()
    ones = jnp.ones((rows, 128), BF16)
    for c in range(0, width, 128):
        queries = k.qkv[m, :, c : c + 128]
        keys = k.qkv[m, :, width + c : width + c + 128]
        values = jnp.concatenate([k.qkv[m, :, 2 * width + c : 2 * width + c + 128], ones], axis=1)
        sums = []
        for half, mask in enumerate((low, high)):
            scores = nt(queries * (mask * jnp.asarray(HEAD_DIM**-0.5, BF16)), keys) + key_bias
            top = jnp.max(scores, axis=-1, keepdims=True)
            raised = jnp.exp(scores - top).astype(BF16)
            k.p[m, c // HEAD_DIM + half] = raised
            sums.append(nn(raised, values))
        inverse_sum = 1.0 / jnp.where(first, sums[0][:, 128:], sums[1][:, 128:])
        k.pool[pool_rows(k, RL, m), c : c + 128] = inverse_sum
        joined = jnp.where(first, sums[0][:, :128], sums[1][:, :128]) * inverse_sum
        k.pool[pool_rows(k, OF, m), c : c + 128] = joined
        k.o[m, :, c : c + 128] = joined.astype(BF16)
    attended = k.o[m]
    mid = pool_rows(k, MID)
    for c in range(0, width, 256):
        k.pool[mid, c : c + 256] = k.x[m, :, c : c + 256].astype(F32) + (
            nn(attended, k.wout[:, c : c + 256]) + vec[:, 4 * width + c : 4 * width + c + 256]
        )
    unit, inverse = normalize(k.pool[mid, :])
    k.n2[m] = unit.astype(BF16)
    k.r2[m] = jnp.broadcast_to(inverse, (rows, 128))
    k.a2[m, z] = (unit * (1.0 + vec[:, 5 * width : 6 * width]) + vec[:, 6 * width : 7 * width]).astype(BF16)


def forward_mlp(k, m, z):
    width = k.x.shape[2]
    vec = k.vec
    normed = k.a2[m, z]
    for c in range(0, k.wup.shape[1], 256):
        u = nn(normed, k.wup[:, c : c + 256]) + vec[:, 8 * width + c : 8 * width + c + 256]
        value, slope = gelu_pair(u)
        k.wide[:, c : c + 256] = value.astype(BF16)
        k.gp[m, :, c : c + 256] = slope.astype(BF16)
    added = nn(k.wide[...], k.wdown[...]) + vec[:, 7 * width : 8 * width]
    k.y[m] = (k.pool[pool_rows(k, MID), :] + added).astype(BF16)


def add_sums(ref, at, value):
    ref[:, at : at + value.shape[1]] += jnp.sum(value, axis=0, keepdims=True)


def backward_mlp(k, gvec, m, z):
    width = k.x.shape[2]
    vec = k.vec
    grad = k.e[m, z]
    add_sums(gvec, 7 * width, grad.astype(F32))
    for c in range(0, k.wup.shape[1], 256):
        grad_up = (
            nt(grad, k.wdown[c : c + 256, :]) * k.gp[m, :, c : c + 256].astype(F32)
        ).astype(BF16)
        k.du[m, :, c : c + 256] = grad_up
        add_sums(gvec, 8 * width + c, grad_up.astype(F32))
    grad_two = nt(k.du[m], k.wup[...])
    unit = k.n2[m].astype(F32)
    add_sums(gvec, 5 * width, grad_two * unit)
    add_sums(gvec, 6 * width, grad_two)
    grad_mid = k.e[m, z].astype(F32) + norm_back(
        grad_two * (1.0 + vec[:, 5 * width : 6 * width]), unit, k.r2[m, :, :1]
    )
    k.pool[pool_rows(k, MID), :] = grad_mid
    branch = grad_mid.astype(BF16)
    k.x[m] = branch
    add_sums(gvec, 4 * width, branch.astype(F32))


def backward_out(k, m):
    k.do[...] = (nt(k.x[m], k.wout[...]) * k.pool[pool_rows(k, RL, m), :]).astype(BF16)
    product = k.do[...].astype(F32) * k.pool[pool_rows(k, OF, m), :]
    k.doo[...] = product.astype(BF16)
    k.rest[...] = (product - k.doo[...].astype(F32)).astype(BF16)


def backward_heads(k, gvec, m):
    rows, width = k.x.shape[1:]
    low, high, first = pair_masks()
    minus = jnp.full((rows, 128), -1.0, BF16)
    scale = HEAD_DIM**-0.5
    for c in range(0, width, 128):
        queries = k.qkv[m, :, c : c + 128]
        keys = k.qkv[m, :, width + c : width + c + 128]
        values = jnp.concatenate([k.qkv[m, :, 2 * width + c : 2 * width + c + 128], minus], axis=1)
        grads = k.do[:, c : c + 128]
        inner = k.doo[:, c : c + 128]
        rest = pltpu.roll(k.rest[:, c : c + 128].astype(F32), HEAD_DIM, 1).astype(BF16)
        inners = (jnp.where(first, inner, rest), jnp.where(first, rest, inner))
        total_q = total_k = total_v = 0.0
        for half, mask in enumerate((low, high)):
            raised = k.p[m, c // HEAD_DIM + half]
            left = jnp.concatenate([grads * mask, inners[half]], axis=1)
            grad_scores = (raised.astype(F32) * nt(left, values)).astype(BF16)
            total_v = total_v + tn(raised, grads * mask)
            total_q = total_q + nn(grad_scores, keys * mask)
            total_k = total_k + tn(grad_scores, queries * mask)
        grad_q = (total_q * scale).astype(BF16)
        grad_v = total_v.astype(BF16)
        k.dp[m, :, c : c + 128] = grad_q
        k.dp[m, :, width + c : width + c + 128] = (total_k * scale).astype(BF16)
        k.dp[m, :, 2 * width + c : 2 * width + c + 128] = grad_v
        add_sums(gvec, 2 * width + c, grad_q.astype(F32))
        add_sums(gvec, 3 * width + c, grad_v.astype(F32))


def backward_qkv(k, gvec, m):
    width = k.x.shape[2]
    grad_one = nt(k.dp[m], k.wqkv[...])
    unit = k.n1[m].astype(F32)
    add_sums(gvec, 0, grad_one * unit)
    add_sums(gvec, width, grad_one)
    grad_in = k.pool[pool_rows(k, MID), :] + norm_back(
        grad_one * (1.0 + k.vec[:, :width]), unit, k.r1[m, :, :1]
    )
    k.ig[m] = grad_in
    k.y[m] = grad_in.astype(BF16)


def out_weight_grad(k):
    micro, rows, width = k.x.shape
    both = micro * rows
    k.wout[...] = tn(k.o[...].reshape(both, width), k.x[...].reshape(both, width)).astype(BF16)


def qkv_weight_grads(k, after_chunk):
    micro, rows, width = k.x.shape
    both = micro * rows
    normed = k.a1[...].reshape(both, width)
    for part in range(3):
        grads = k.dp[:, :, part * width : (part + 1) * width].reshape(both, width)
        k.wqkv[:, part * width : (part + 1) * width] = tn(normed, grads).astype(BF16)
        after_chunk(part)


def mlp_weight_grads(k, origin, start, fresh):
    micro, rows, width = k.x.shape
    both = micro * rows
    normed = k.a2[:, origin].reshape(both, width)
    grad = k.e[:, origin].reshape(both, width)
    for c in range(0, width, 256):
        at = pl.ds(pl.multiple_of(start + c, 256), 256)
        u = nn(normed, k.wup[:, at]) + k.vec[:, pl.ds(pl.multiple_of(8 * width + start + c, 256), 256)]
        value, slope = gelu_pair(u)
        grad_up = (nt(grad, k.wdown[at, :]) * slope).astype(BF16)
        up = tn(normed, grad_up)
        down = tn(value.astype(BF16), grad)
        if fresh:
            k.pool[:width, c : c + 256] = up
            k.pool[width + c : width + c + 256, :] = down
        else:
            k.pool[:width, c : c + 256] += up
            k.pool[width + c : width + c + 256, :] += down


def own_weight_grads(k, z, rows_at, down_at):
    micro, rows, width = k.x.shape
    both = micro * rows
    normed = k.a2[:, z].reshape(both, width)
    picked = k.a2[:, z, :, rows_at].reshape(both, UP_ROWS)
    grad = k.e[:, z].reshape(both, width)
    for c in range(0, width, 256):
        at = pl.ds(pl.multiple_of(z * width + c, 256), 256)
        bias = k.vec[:, pl.ds(pl.multiple_of(8 * width + z * width + c, 256), 256)]
        value, _ = gelu_pair(nn(normed, k.wup[:, at]) + bias)
        k.pool[down_at + c : down_at + c + 256, :] = tn(value.astype(BF16), grad)
    for c in range(0, k.wup.shape[1], width):
        at = c // width * UP_ROWS
        grads = k.du[:, :, c : c + width].reshape(both, width)
        k.pool[at : at + UP_ROWS, :] = tn(picked, grads)


def slice_weight_grads(k, origin, piece, rows_at, down_at):
    micro, rows, width = k.x.shape
    both = micro * rows
    normed = k.a2[:, origin].reshape(both, width)
    picked = k.a2[:, origin, :, rows_at].reshape(both, UP_ROWS)
    grad = k.e[:, origin].reshape(both, width)
    up_at = pl.ds(pl.multiple_of(piece * UP_ROWS, UP_ROWS), UP_ROWS)
    for c in range(0, width, 256):
        at = pl.ds(pl.multiple_of(piece * width + c, 256), 256)
        bias = k.vec[:, pl.ds(pl.multiple_of(8 * width + piece * width + c, 256), 256)]
        value, slope = gelu_pair(nn(normed, k.wup[:, at]) + bias)
        grad_up = (nt(grad, k.wdown[at, :]) * slope).astype(BF16)
        k.pool[up_at, c : c + 256] += tn(picked, grad_up)
        if down_at is not None:
            k.pool[down_at + c : down_at + c + 256, :] += tn(value.astype(BF16), grad)


def pipeline_kernel(scratch_names, fused, *refs):
    k = Refs(INPUTS + RESULTS + scratch_names, refs)
    sec = lax.axis_index("section")
    count = lax.axis_size("section")
    peers = lax.axis_size("dp")
    me = lax.axis_index("dp")
    micro, rows, width = k.x.shape
    hidden = k.wup.shape[1]
    chips = k.e.shape[1]
    z, core = (me // 2, me % 2) if fused else (0, 0)
    gvec = k.gvec if fused else k.vector_grad
    share = width // peers
    is_first = sec == 0
    is_last = sec == count - 1
    not_last = sec < count - 1
    after = jnp.minimum(sec + 1, count - 1)
    before = jnp.maximum(sec - 1, 0)

    barrier = pltpu.get_barrier_semaphore()

    @pl.when(sec > 0)
    def _():
        pl.semaphore_signal(barrier, inc=1, device_id={"section": before}, device_id_type=MESH)

    @pl.when(not_last)
    def _():
        pl.semaphore_signal(barrier, inc=1, device_id={"section": after}, device_id_type=MESH)

    if fused:
        for step in range(1, peers):
            pl.semaphore_signal(
                barrier, inc=1, device_id={"dp": (me + step) % peers}, device_id_type=MESH
            )

    def patch_copy(m):
        return pltpu.make_async_copy(k.patches.at[m], k.x.at[m], k.psem.at[m])

    def cot_copy(m):
        return pltpu.make_async_copy(k.cot.at[m], k.e.at[m, z], k.csem.at[m])

    loads = [
        pltpu.make_async_copy(src.at[0], dst, k.wsem.at[i])
        for i, (src, dst) in enumerate(
            ((k.wqkv_h, k.wqkv), (k.wout_h, k.wout), (k.wup_h, k.wup), (k.wdown_h, k.wdown))
        )
    ]

    @pl.when(is_first)
    def _():
        for m in range(micro):
            patch_copy(m).start()

    lens_copy = pltpu.make_async_copy(k.lengths, k.lens, k.lsem.at[0])
    lens_copy.start()
    loads[0].start()
    loads[1].start()

    @pl.when(is_last)
    def _():
        for m in range(micro):
            cot_copy(m).start()

    k.bias[:, :width] = k.vec[:, 2 * width : 3 * width]
    k.bias[:, width : 2 * width] = jnp.zeros((1, width), F32)
    k.bias[:, 2 * width :] = k.vec[:, 3 * width : 4 * width]
    gvec[...] = jnp.zeros_like(gvec)
    lens_copy.wait()
    loads[0].wait()
    loads[1].wait()
    loads[2].start()
    loads[3].start()

    def y_send(m):
        return pltpu.make_async_remote_copy(
            src_ref=k.y.at[m], dst_ref=k.x.at[m], send_sem=k.xsend.at[m], recv_sem=k.xrecv.at[m],
            device_id={"section": after}, device_id_type=MESH,
        )

    def e_send(m):
        return pltpu.make_async_remote_copy(
            src_ref=k.y.at[m], dst_ref=k.e.at[m, z], send_sem=k.esend.at[m], recv_sem=k.erecv.at[m],
            device_id={"section": before}, device_id_type=MESH,
        )

    def out_copy(m):
        return pltpu.make_async_copy(k.y.at[m], k.outputs.at[m], k.osem.at[m])

    def in_copy(m):
        return pltpu.make_async_copy(k.ig.at[m], k.input_grads.at[m], k.isem.at[m])

    def to_peer(src, dst, send, recv, device):
        return pltpu.make_async_remote_copy(
            src_ref=src, dst_ref=dst, send_sem=send, recv_sem=recv,
            device_id={"dp": device}, device_id_type=MESH,
        )

    def pass_on(ref, sends, recvs, m, origin, up):
        return to_peer(
            ref.at[m, origin], ref.at[m, origin], sends.at[0 if up else 1, m, origin],
            recvs.at[m, origin], me + 2 if up else me - 2,
        )

    def share_own(ref, sends, recvs, m):
        @pl.when(z < chips - 1)
        def _():
            pass_on(ref, sends, recvs, m, z, True).start()

        @pl.when(z > 0)
        def _():
            pass_on(ref, sends, recvs, m, z, False).start()

    def relay(ref, sends, recvs, m, distance):
        @pl.when(z >= distance)
        def _():
            pass_on(ref, sends, recvs, m, z - distance, True).wait_recv()

            @pl.when(z < chips - 1)
            def _():
                pass_on(ref, sends, recvs, m, z - distance, True).start()

        @pl.when(z + distance < chips)
        def _():
            pass_on(ref, sends, recvs, m, z + distance, False).wait_recv()

            @pl.when(z > 0)
            def _():
                pass_on(ref, sends, recvs, m, z + distance, False).start()

    def settle(ref, sends, recvs, m):
        for distance in range(chips):
            @pl.when((z >= distance) & (z < chips - 1))
            def _():
                pass_on(ref, sends, recvs, m, z - distance, True).wait_send()

            @pl.when((z + distance < chips) & (z > 0))
            def _():
                pass_on(ref, sends, recvs, m, z + distance, False).wait_send()

    if fused:
        acts = (k.a2, k.asend, k.arecv)
        errs = (k.e, k.bsend, k.brecv)
    arrivals = (sec > 0).astype(jnp.int32) + not_last.astype(jnp.int32)
    pl.semaphore_wait(barrier, arrivals + (peers - 1 if fused else 0))

    @pl.when(is_last)
    def _():
        for m in range(micro):
            cot_copy(m).wait()
            valid = lax.broadcasted_iota(jnp.int32, (rows, width), 0) < k.lens[m]
            k.e[m, z] = jnp.where(valid, k.e[m, z].astype(F32), 0.0).astype(BF16)
            if fused:
                share_own(*errs, m)
        if fused:
            for distance in range(1, chips - 1):
                for m in range(micro):
                    relay(*errs, m, distance)

    sibling = me + 1 - 2 * core

    def part_rows(chip, parity):
        return pl.ds(pl.multiple_of(share * (2 * chip + parity), share), share)

    def part_ref(part, chip, parity):
        if part < 3:
            return k.wqkv.at[part_rows(chip, parity), pl.ds(part * width, width)]
        return k.wout.at[part_rows(chip, parity), :]

    def pair_copy(part, chip):
        return to_peer(
            part_ref(part, chip, 1 - core), k.prx.at[part, chip],
            k.pxsend.at[part, chip], k.pxrecv.at[part, chip], sibling,
        )

    def send_pair(part):
        for chip in range(chips):
            pair_copy(part, chip).start()

    ends_first = is_first & not_last if fused else False
    waits_turn = is_first & (core == 1) & not_last

    def forward_step(m):
        @pl.when(is_first)
        def _():
            patch_copy(m).wait()

        @pl.when(sec > 0)
        def _():
            y_send(m).wait_recv()

        key_bias = jnp.where(
            lax.broadcasted_iota(jnp.int32, (1, rows), 1) < k.lens[m], 0.0, -1e30
        )
        forward_attention(k, m, z, key_bias)
        if fused:
            share_own(*acts, m)

            @pl.when(waits_turn & (m > 0))
            def _():
                y_send(m - 1).start()

        @pl.when(m == 0)
        def _():
            loads[2].wait()
            loads[3].wait()

        forward_mlp(k, m, z)

        @pl.when(not_last & jnp.logical_not(waits_turn))
        def _():
            y_send(m).start()

        out_copy(m).start()

    def relay_acts(*distances):
        for distance in distances:
            for m in range(micro):
                relay(*acts, m, distance)

    def backward_step(m):
        out_copy(m).wait()

        @pl.when(not_last)
        def _():
            e_send(m).wait_recv()
            if fused:
                share_own(*errs, m)

        backward_mlp(k, gvec, m, z)
        backward_out(k, m)
        if fused:
            @pl.when(ends_first & (m == micro - 1))
            def _():
                out_weight_grad(k)
                send_pair(3)
                for early in range(micro - 1):
                    relay(*errs, early, 2)

        backward_heads(k, gvec, m)

        backward_qkv(k, gvec, m)

        @pl.when(sec > 0)
        def _():
            e_send(m).start()

        in_copy(m).start()
        if fused:
            @pl.when(ends_first & (m < micro - 1))
            def _():
                relay(*errs, m, 1)

    def turn_round():
        if fused:
            @pl.when(is_first & (core == 0) & not_last)
            def _():
                y_send(micro - 1).wait_send()
                pl.semaphore_signal(k.turn, inc=1, device_id={"dp": me + 1}, device_id_type=MESH)

            @pl.when(waits_turn)
            def _():
                pl.semaphore_wait(k.turn, 1)
                y_send(micro - 1).start()
        for m in range(micro):
            waited = is_first & (core == 0) if fused and m == micro - 1 else False

            @pl.when(jnp.logical_not(waited))
            def _():
                y_send(m).wait_send()

        if fused:
            relay_acts(1)
            pl.when(sec < count - 2)(lambda: relay_acts(*range(2, chips - 1)))

    def step(index, carry):
        forward = jnp.where(is_last, index % 2 == 0, index < micro)
        m = jnp.where(is_last, index // 2, index % micro)
        pl.when(forward)(lambda: forward_step(m))
        pl.when(not_last & (index == micro))(turn_round)
        pl.when(jnp.logical_not(forward))(lambda: backward_step(m))
        return carry

    lax.fori_loop(0, 2 * micro, step, 0)

    def finish_hops():
        for m in range(micro):
            in_copy(m).wait()

            @pl.when(sec > 0)
            def _():
                e_send(m).wait_send()

    if not fused:
        out_weight_grad(k)
        qkv_weight_grads(k, lambda part: None)
        for c in range(0, hidden, width):
            mlp_weight_grads(k, 0, c, True)
            k.wup[:, c : c + width] = k.pool[:width, :].astype(BF16)
            k.wdown[c : c + width, :] = k.pool[width:, :].astype(BF16)
        copies = [
            pltpu.make_async_copy(src, dst, k.wsem.at[i])
            for i, (src, dst) in enumerate(
                ((k.wqkv, k.qkv_grad), (k.wout, k.out_grad), (k.wup, k.up_grad), (k.wdown, k.down_grad))
            )
        ]
        for copy in copies:
            copy.start()
        for copy in copies:
            copy.wait()
        finish_hops()
        return

    @pl.when(jnp.logical_not(ends_first))
    def _():
        out_weight_grad(k)
        send_pair(3)

    qkv_weight_grads(k, send_pair)

    length = gvec.shape[1] // peers

    def vector_copy(step):
        device = (me + step) % peers
        return to_peer(
            gvec.at[:, pl.ds(pl.multiple_of(device * length, 128), length)], k.vrx.at[step],
            k.vsend.at[step], k.vrecv.at[step], device,
        )

    for step in range(1, peers):
        vector_copy(step).start()

    def chain_copy(up, part, place):
        chip = place if up else chips - 1 - place
        lane = 0 if up else 1
        return to_peer(
            part_ref(part, chip, core), k.rsx.at[lane, part, place - 1],
            k.rsend.at[lane, part, place], k.rrecv.at[lane, part, place],
            me + 2 if up else me - 2,
        )

    def chain(stage, place, parts=range(4)):
        for up in (True, False):
            @pl.when((z if up else chips - 1 - z) == stage)
            def _():
                chip = place if up else chips - 1 - place
                for part in parts:
                    if stage > 0:
                        chain_copy(up, part, place).wait_recv()
                        target = part_ref(part, chip, core)
                        target[...] = (
                            target[...].astype(F32)
                            + k.rsx[0 if up else 1, part, place - 1].astype(F32)
                        ).astype(BF16)
                    chain_copy(up, part, place).start()

    for part in (3, 0, 1, 2):
        for chip in range(chips):
            pair_copy(part, chip).wait()
            target = part_ref(part, chip, core)
            target[...] = (target[...].astype(F32) + k.prx[part, chip].astype(F32)).astype(BF16)
        chain(0, chips - 1, (part,))

    def follow(place):
        for up in (True, False):
            @pl.when((z if up else chips - 1 - z) == 0)
            def _():
                for part in range(4):
                    chain_copy(up, part, place + 1).wait_send()
                for part in range(4):
                    chain_copy(up, part, place).start()

    @pl.when(not_last & (sec > 0))
    def _():
        for early in range(micro - 1):
            relay(*errs, early, 1)

    @pl.when(not_last)
    def _():
        relay(*errs, micro - 1, 1)

    @pl.when(not_last & (sec > 0))
    def _():
        for early in range(micro - 1):
            relay(*errs, early, 2)

    pl.when(is_last)(lambda: relay_acts(1))
    pl.when(sec >= count - 2)(lambda: relay_acts(*range(2, chips - 1)))
    def nearby(index):
        low = z + (index % 2) * (1 - 2 * (z % 2))
        return low + (index // 2) * (2 - 4 * ((low // 2) % 2))

    rows_at = pl.ds(pl.multiple_of(128 * ((3 * z) // 2), 128), UP_ROWS)
    down_base = chips * UP_ROWS

    def batch(origin):
        slice_weight_grads(k, origin, z, rows_at, down_base)

        def other(step, carry):
            slice_weight_grads(k, origin, (z + step) % chips, rows_at, None)
            return carry

        lax.fori_loop(1, chips, other, 0)

    inner = (z > 0) & (z < chips - 1)

    @pl.when(not_last & inner)
    def _():
        relay(*errs, micro - 1, 2)

    own_weight_grads(k, z, rows_at, down_base)
    follow(2)
    chain(1, 3, (3, 0, 1, 2))

    @pl.when(not_last & jnp.logical_not(inner))
    def _():
        relay(*errs, micro - 1, 2)

    batch(nearby(1))
    chain(1, 2)
    batch(nearby(2))
    follow(1)
    chain(2, 3, (3, 0, 1, 2))
    for m in range(micro):
        relay(*acts, m, chips - 1)
        relay(*errs, m, chips - 1)
    batch(nearby(3))

    per_core = hidden // peers

    def down_rows(parity):
        return pl.ds(pl.multiple_of(down_base + per_core * parity, 128), per_core)

    def up_rows(piece, parity):
        first_row = UP_ROWS * piece + (UP_ROWS - 2 * share) * (z % 2) + share * parity
        return pl.ds(pl.multiple_of(first_row, 32), share)

    for piece in range(chips):
        k.upx[piece] = k.pool[up_rows(piece, 1 - core), :].astype(BF16)
    up_pair = to_peer(k.upx, k.uprx, k.upsem.at[0], k.upsem.at[1], sibling)
    up_pair.start()
    k.dnx[...] = k.pool[down_rows(1 - core), :].astype(BF16)
    down_pair = to_peer(k.dnx, k.dnrx, k.dnsem.at[0], k.dnsem.at[1], sibling)
    down_pair.start()
    finals = []
    up_pair.wait()
    for piece in range(chips):
        at = up_rows(piece, core)
        k.pool[at, :] += k.uprx[piece].astype(F32)
        final = pltpu.make_async_copy(
            k.pool.at[at], k.up_grad.at[:, pl.ds(piece * width, width)], k.gsem.at[5 + piece]
        )
        final.start()
        finals.append(final)
    down_pair.wait()
    k.pool[down_rows(core), :] += k.dnrx[...].astype(F32)
    final = pltpu.make_async_copy(k.pool.at[down_rows(core)], k.down_grad, k.gsem.at[0])
    final.start()
    finals.append(final)
    finish_hops()

    for part in range(4):
        held = k.ig.at[part // 2, pl.ds(share * (part % 2), share)]
        held[...] = part_ref(part, z, core)[...].astype(F32)

        @pl.when(z > 0)
        def _():
            chain_copy(True, part, z).wait_recv()
            held[...] += k.rsx[0, part, z - 1].astype(F32)

        @pl.when(z < chips - 1)
        def _():
            chain_copy(False, part, chips - 1 - z).wait_recv()
            held[...] += k.rsx[1, part, chips - 2 - z].astype(F32)

        target = k.qkv_grad.at[:, pl.ds(part * width, width)] if part < 3 else k.out_grad
        final = pltpu.make_async_copy(held, target, k.gsem.at[1 + part])
        final.start()
        finals.append(final)
    own = gvec[:, pl.ds(pl.multiple_of(me * length, 128), length)]
    for step in range(1, peers):
        vector_copy(step).wait()
        own = own + k.vrx[step]
    k.vector_grad[...] = own

    for m in range(micro):
        settle(*acts, m)
        settle(*errs, m)
    for part in range(4):
        for up in (True, False):
            for place in range(1, chips):
                position = z if up else chips - 1 - z

                @pl.when((position < place) & ((position > 0) | (place == 1)))
                def _():
                    chain_copy(up, part, place).wait_send()
    for final in finals:
        final.wait()


def deliver_kernel(count, *refs):
    sources, targets, held = refs[:count], refs[count : 2 * count], refs[2 * count : 3 * count]
    sems = refs[-1]
    fetches = [
        pltpu.make_async_copy(sources[i], held[i], sems.at[0, i]) for i in range(count)
    ]
    stores = [
        pltpu.make_async_copy(held[i], targets[i], sems.at[1, i]) for i in range(count)
    ]
    for fetch in fetches:
        fetch.start()
    for fetch, store in zip(fetches, stores):
        fetch.wait()
        store.start()
    for store in stores:
        store.wait()


def deliver(arrays):
    anywhere = pl.BlockSpec(memory_space=pl.ANY)
    count = len(arrays)
    return pl.pallas_call(
        partial(deliver_kernel, count),
        out_shape=tuple(jax.ShapeDtypeStruct(a.shape, a.dtype) for a in arrays),
        in_specs=[anywhere] * count,
        out_specs=(anywhere,) * count,
        scratch_shapes=[pltpu.VMEM(a.shape, a.dtype) for a in arrays]
        + [pltpu.SemaphoreType.DMA((2, count))],
        compiler_params=pltpu.CompilerParams(vmem_limit_bytes=62 << 20),
    )(*arrays)


def shards(patches, lengths, qkv_weight, out_weight, up_weight, down_weight, vectors, cotangent):
    micro, _, rows, width = patches.shape
    hidden = up_weight.shape[2]
    peers = lax.axis_size("dp")
    fused = peers == 8 and hidden == peers // 2 * width and 4 * (width // peers) == 3 * 128
    chips = peers // 2 if fused else 1
    plan = scratch_plan(micro, rows, width, hidden, chips, peers, fused)
    anywhere = pl.BlockSpec(memory_space=pl.ANY)
    in_vmem = pl.BlockSpec(memory_space=pltpu.VMEM)
    kept = F32 if fused else BF16
    cut = peers if fused else 1
    results = pl.pallas_call(
        partial(pipeline_kernel, tuple(plan), fused),
        out_shape=(
            jax.ShapeDtypeStruct((micro, rows, width), BF16),
            jax.ShapeDtypeStruct((micro, rows, width), F32),
            jax.ShapeDtypeStruct((width // cut, 3 * width), kept),
            jax.ShapeDtypeStruct((width // cut, width), kept),
            jax.ShapeDtypeStruct((width // cut, hidden), kept),
            jax.ShapeDtypeStruct((hidden // cut, width), kept),
            jax.ShapeDtypeStruct((1, vectors.shape[1] // cut), F32),
        ),
        in_specs=[
            anywhere,
            anywhere,
            anywhere,
            anywhere,
            anywhere,
            anywhere,
            in_vmem,
            anywhere,
        ],
        out_specs=(anywhere,) * 6 + (in_vmem,),
        scratch_shapes=list(plan.values()),
        compiler_params=pltpu.CompilerParams(
            collective_id=0, has_side_effects=True, vmem_limit_bytes=62 << 20
        ),
    )(
        patches[:, 0],
        lengths[:, 0],
        qkv_weight,
        out_weight,
        up_weight,
        down_weight,
        vectors,
        cotangent[:, 0],
    )
    if fused:
        results = deliver(results)
    outputs, input_grads, *grads, vector_grad = results
    if fused:
        grads = [grad[None] for grad in grads]
    else:
        grads = [
            lax.psum_scatter(grad[None], "dp", scatter_dimension=1, tiled=True).astype(F32)
            for grad in grads
        ]
        vector_grad = lax.psum_scatter(vector_grad, "dp", scatter_dimension=1, tiled=True)
    return (outputs[None, :, None], input_grads[None, :, None], *grads, vector_grad)


def solution(mesh):
    placed = (
        P(None, "dp", None, None),
        P(None, "dp"),
        P("section", None, None),
        P("section", None, None),
        P("section", None, None),
        P("section", None, None),
        P("section", None),
        P(None, "dp", None, None),
    )
    return jax.shard_map(
        shards,
        mesh=mesh,
        in_specs=placed,
        out_specs=(
            P("section", None, "dp", None, None),
            P("section", None, "dp", None, None),
            P("section", "dp", None),
            P("section", "dp", None),
            P("section", "dp", None),
            P("section", "dp", None),
            P("section", "dp"),
        ),
        check_vma=False,
    )
```

```python
from functools import partial

import jax
import jax.numpy as jnp
from jax import lax
from jax.experimental import pallas as pl
from jax.experimental.pallas import tpu as pltpu
from jax.sharding import PartitionSpec as P

HEAD_DIM = 64
EPS = 1e-06
F32 = jnp.float32
BF16 = jnp.bfloat16
MESH = pl.DeviceIdType.MESH


def nn(left, right):
    return jnp.dot(left, right, preferred_element_type=F32)


def nt(left, right):
    return lax.dot_general(left, right, (((1,), (1,)), ((), ())), preferred_element_type=F32)


def tn(left, right):
    return lax.dot_general(left, right, (((0,), (0,)), ((), ())), preferred_element_type=F32)


def normalize(hidden):
    centered = hidden - jnp.mean(hidden, axis=-1, keepdims=True)
    inverse = lax.rsqrt(jnp.mean(centered * centered, axis=-1, keepdims=True) + EPS)
    return centered * inverse, inverse


def norm_back(grad, unit, inverse):
    average = jnp.mean(grad, axis=-1, keepdims=True)
    slope = jnp.mean(grad * unit, axis=-1, keepdims=True)
    return inverse * (grad - average - unit * slope)


def gelu_pair(u):
    phi = 0.5 + 0.5 * lax.erf(u * 0.7071067811865476)
    density = jnp.exp(u * u * -0.5) * 0.3989422804014327
    return u * phi, phi + u * density


class Refs:
    def __init__(self, names, refs):
        self.__dict__.update(zip(names, refs))


INPUTS = ("patches", "lengths", "wqkv_h", "wout_h", "wup_h", "wdown_h", "vec", "cot")
RESULTS = ("outputs", "input_grads", "qkv_grad", "out_grad", "up_grad", "down_grad", "vector_grad")


def scratch_plan(micro, rows, width, hidden, chips, peers, fused):
    heads = width // HEAD_DIM
    dma = pltpu.SemaphoreType.DMA
    vm = pltpu.VMEM
    act = vm((micro, rows, width), BF16)
    blocks = vm((micro, chips, rows, width), BF16)
    plan = dict(
        wqkv=vm((width, 3 * width), BF16),
        wout=vm((width, width), BF16),
        wup=vm((width, hidden), BF16),
        wdown=vm((hidden, width), BF16),
        x=act, a1=act, n1=act, o=act, n2=act, y=act, a2=blocks, e=blocks,
        r1=vm((micro, rows, 128), F32),
        r2=vm((micro, rows, 128), F32),
        qkv=vm((micro, rows, 3 * width), BF16),
        bias=vm((1, 3 * width), F32),
        p=vm((micro, heads, rows, rows), BF16),
        wide=vm((rows, hidden), BF16),
        gp=vm((micro, rows, hidden), BF16),
        du=vm((micro, rows, hidden), BF16),
        dp=vm((micro, rows, 3 * width), BF16),
        do=vm((rows, width), BF16),
        doo=vm((rows, width), BF16),
        rest=vm((rows, width), BF16),
        pool=vm((chips * UP_ROWS + width, width) if fused else (2 * width, width), F32),
        ig=vm((micro, rows, width), F32),
        lens=pltpu.SMEM((micro,), jnp.int32),
        lsem=dma((1,)),
        wsem=dma((4,)),
        psem=dma((micro,)),
        csem=dma((micro,)),
        xsend=dma((micro,)),
        xrecv=dma((micro,)),
        esend=dma((micro,)),
        erecv=dma((micro,)),
        osem=dma((micro,)),
        isem=dma((micro,)),
        gsem=dma((3 * chips,)),
    )
    if fused:
        share = width // peers
        plan.update(
            gvec=vm((1, 8 * width + hidden), F32),
            asend=dma((2, micro, chips)),
            arecv=dma((micro, chips)),
            bsend=dma((2, micro, chips)),
            brecv=dma((micro, chips)),
            prx=vm((4, chips, share, width), BF16),
            pxsend=dma((4, chips)),
            pxrecv=dma((4, chips)),
            rsx=vm((2, 4, chips - 1, share, width), BF16),
            rsend=dma((2, 4, chips)),
            rrecv=dma((2, 4, chips)),
            vrx=vm((peers, 1, (8 * width + hidden) // peers), F32),
            vsend=dma((peers,)),
            vrecv=dma((peers,)),
            upx=vm((chips, share, width), BF16),
            uprx=vm((chips, share, width), BF16),
            upsem=dma((2,)),
            dnx=vm((hidden // peers, width), BF16),
            dnrx=vm((hidden // peers, width), BF16),
            dnsem=dma((2,)),
            turn=pltpu.SemaphoreType.REGULAR,
        )
    return plan


def pair_masks():
    lane = lax.broadcasted_iota(jnp.int32, (1, 128), 1)
    return (lane < HEAD_DIM).astype(BF16), (lane >= HEAD_DIM).astype(BF16), lane < HEAD_DIM


def pool_rows(k, block, m=0):
    rows = k.x.shape[1]
    return pl.ds(pl.multiple_of((block + m) * rows, rows), rows)


RL, OF, MID = 0, 2, 4
UP_ROWS = 256


def forward_attention(k, m, z, key_bias):
    rows, width = k.x.shape[1:]
    vec = k.vec
    unit, inverse = normalize(k.x[m].astype(F32))
    k.n1[m] = unit.astype(BF16)
    k.r1[m] = jnp.broadcast_to(inverse, (rows, 128))
    k.a1[m] = (unit * (1.0 + vec[:, :width]) + vec[:, width : 2 * width]).astype(BF16)
    normed = k.a1[m]
    for c in range(0, 3 * width, 256):
        k.qkv[m, :, c : c + 256] = (nn(normed, k.wqkv[:, c : c + 256]) + k.bias[:, c : c + 256]).astype(BF16)
    low, high, first = pair_masks()
    ones = jnp.ones((rows, 128), BF16)
    for c in range(0, width, 128):
        queries = k.qkv[m, :, c : c + 128]
        keys = k.qkv[m, :, width + c : width + c + 128]
        values = jnp.concatenate([k.qkv[m, :, 2 * width + c : 2 * width + c + 128], ones], axis=1)
        sums = []
        for half, mask in enumerate((low, high)):
            scores = nt(queries * (mask * jnp.asarray(HEAD_DIM**-0.5, BF16)), keys) + key_bias
            top = jnp.max(scores, axis=-1, keepdims=True)
            raised = jnp.exp(scores - top).astype(BF16)
            k.p[m, c // HEAD_DIM + half] = raised
            sums.append(nn(raised, values))
        inverse_sum = 1.0 / jnp.where(first, sums[0][:, 128:], sums[1][:, 128:])
        k.pool[pool_rows(k, RL, m), c : c + 128] = inverse_sum
        joined = jnp.where(first, sums[0][:, :128], sums[1][:, :128]) * inverse_sum
        k.pool[pool_rows(k, OF, m), c : c + 128] = joined
        k.o[m, :, c : c + 128] = joined.astype(BF16)
    attended = k.o[m]
    mid = pool_rows(k, MID)
    for c in range(0, width, 256):
        k.pool[mid, c : c + 256] = k.x[m, :, c : c + 256].astype(F32) + (
            nn(attended, k.wout[:, c : c + 256]) + vec[:, 4 * width + c : 4 * width + c + 256]
        )
    unit, inverse = normalize(k.pool[mid, :])
    k.n2[m] = unit.astype(BF16)
    k.r2[m] = jnp.broadcast_to(inverse, (rows, 128))
    k.a2[m, z] = (unit * (1.0 + vec[:, 5 * width : 6 * width]) + vec[:, 6 * width : 7 * width]).astype(BF16)


def forward_mlp(k, m, z):
    width = k.x.shape[2]
    vec = k.vec
    normed = k.a2[m, z]
    for c in range(0, k.wup.shape[1], 256):
        u = nn(normed, k.wup[:, c : c + 256]) + vec[:, 8 * width + c : 8 * width + c + 256]
        value, slope = gelu_pair(u)
        k.wide[:, c : c + 256] = value.astype(BF16)
        k.gp[m, :, c : c + 256] = slope.astype(BF16)
    added = nn(k.wide[...], k.wdown[...]) + vec[:, 7 * width : 8 * width]
    k.y[m] = (k.pool[pool_rows(k, MID), :] + added).astype(BF16)


def add_sums(ref, at, value):
    ref[:, at : at + value.shape[1]] += jnp.sum(value, axis=0, keepdims=True)


def backward_mlp(k, gvec, m, z):
    width = k.x.shape[2]
    vec = k.vec
    grad = k.e[m, z]
    add_sums(gvec, 7 * width, grad.astype(F32))
    for c in range(0, k.wup.shape[1], 256):
        grad_up = (
            nt(grad, k.wdown[c : c + 256, :]) * k.gp[m, :, c : c + 256].astype(F32)
        ).astype(BF16)
        k.du[m, :, c : c + 256] = grad_up
        add_sums(gvec, 8 * width + c, grad_up.astype(F32))
    grad_two = nt(k.du[m], k.wup[...])
    unit = k.n2[m].astype(F32)
    add_sums(gvec, 5 * width, grad_two * unit)
    add_sums(gvec, 6 * width, grad_two)
    grad_mid = k.e[m, z].astype(F32) + norm_back(
        grad_two * (1.0 + vec[:, 5 * width : 6 * width]), unit, k.r2[m, :, :1]
    )
    k.pool[pool_rows(k, MID), :] = grad_mid
    branch = grad_mid.astype(BF16)
    k.x[m] = branch
    add_sums(gvec, 4 * width, branch.astype(F32))


def backward_out(k, m):
    k.do[...] = (nt(k.x[m], k.wout[...]) * k.pool[pool_rows(k, RL, m), :]).astype(BF16)
    product = k.do[...].astype(F32) * k.pool[pool_rows(k, OF, m), :]
    k.doo[...] = product.astype(BF16)
    k.rest[...] = (product - k.doo[...].astype(F32)).astype(BF16)


def backward_heads(k, gvec, m):
    rows, width = k.x.shape[1:]
    low, high, first = pair_masks()
    minus = jnp.full((rows, 128), -1.0, BF16)
    scale = HEAD_DIM**-0.5
    for c in range(0, width, 128):
        queries = k.qkv[m, :, c : c + 128]
        keys = k.qkv[m, :, width + c : width + c + 128]
        values = jnp.concatenate([k.qkv[m, :, 2 * width + c : 2 * width + c + 128], minus], axis=1)
        grads = k.do[:, c : c + 128]
        inner = k.doo[:, c : c + 128]
        rest = pltpu.roll(k.rest[:, c : c + 128].astype(F32), HEAD_DIM, 1).astype(BF16)
        inners = (jnp.where(first, inner, rest), jnp.where(first, rest, inner))
        total_q = total_k = total_v = 0.0
        for half, mask in enumerate((low, high)):
            raised = k.p[m, c // HEAD_DIM + half]
            left = jnp.concatenate([grads * mask, inners[half]], axis=1)
            grad_scores = (raised.astype(F32) * nt(left, values)).astype(BF16)
            total_v = total_v + tn(raised, grads * mask)
            total_q = total_q + nn(grad_scores, keys * mask)
            total_k = total_k + tn(grad_scores, queries * mask)
        grad_q = (total_q * scale).astype(BF16)
        grad_v = total_v.astype(BF16)
        k.dp[m, :, c : c + 128] = grad_q
        k.dp[m, :, width + c : width + c + 128] = (total_k * scale).astype(BF16)
        k.dp[m, :, 2 * width + c : 2 * width + c + 128] = grad_v
        add_sums(gvec, 2 * width + c, grad_q.astype(F32))
        add_sums(gvec, 3 * width + c, grad_v.astype(F32))


def backward_qkv(k, gvec, m):
    width = k.x.shape[2]
    grad_one = nt(k.dp[m], k.wqkv[...])
    unit = k.n1[m].astype(F32)
    add_sums(gvec, 0, grad_one * unit)
    add_sums(gvec, width, grad_one)
    grad_in = k.pool[pool_rows(k, MID), :] + norm_back(
        grad_one * (1.0 + k.vec[:, :width]), unit, k.r1[m, :, :1]
    )
    k.ig[m] = grad_in
    k.y[m] = grad_in.astype(BF16)


def out_weight_grad(k):
    micro, rows, width = k.x.shape
    both = micro * rows
    k.wout[...] = tn(k.o[...].reshape(both, width), k.x[...].reshape(both, width)).astype(BF16)


def qkv_weight_grads(k, after_chunk):
    micro, rows, width = k.x.shape
    both = micro * rows
    normed = k.a1[...].reshape(both, width)
    for part in range(3):
        grads = k.dp[:, :, part * width : (part + 1) * width].reshape(both, width)
        k.wqkv[:, part * width : (part + 1) * width] = tn(normed, grads).astype(BF16)
        after_chunk(part)


def mlp_weight_grads(k, origin, start, fresh):
    micro, rows, width = k.x.shape
    both = micro * rows
    normed = k.a2[:, origin].reshape(both, width)
    grad = k.e[:, origin].reshape(both, width)
    for c in range(0, width, 256):
        at = pl.ds(pl.multiple_of(start + c, 256), 256)
        u = nn(normed, k.wup[:, at]) + k.vec[:, pl.ds(pl.multiple_of(8 * width + start + c, 256), 256)]
        value, slope = gelu_pair(u)
        grad_up = (nt(grad, k.wdown[at, :]) * slope).astype(BF16)
        up = tn(normed, grad_up)
        down = tn(value.astype(BF16), grad)
        if fresh:
            k.pool[:width, c : c + 256] = up
            k.pool[width + c : width + c + 256, :] = down
        else:
            k.pool[:width, c : c + 256] += up
            k.pool[width + c : width + c + 256, :] += down


def own_weight_grads(k, z, rows_at, down_at):
    micro, rows, width = k.x.shape
    both = micro * rows
    normed = k.a2[:, z].reshape(both, width)
    picked = k.a2[:, z, :, rows_at].reshape(both, UP_ROWS)
    grad = k.e[:, z].reshape(both, width)
    for c in range(0, width, 256):
        at = pl.ds(pl.multiple_of(z * width + c, 256), 256)
        bias = k.vec[:, pl.ds(pl.multiple_of(8 * width + z * width + c, 256), 256)]
        value, _ = gelu_pair(nn(normed, k.wup[:, at]) + bias)
        k.pool[down_at + c : down_at + c + 256, :] = tn(value.astype(BF16), grad)
    for c in range(0, k.wup.shape[1], width):
        at = c // width * UP_ROWS
        grads = k.du[:, :, c : c + width].reshape(both, width)
        k.pool[at : at + UP_ROWS, :] = tn(picked, grads)


def slice_weight_grads(k, origin, piece, rows_at, down_at):
    micro, rows, width = k.x.shape
    both = micro * rows
    normed = k.a2[:, origin].reshape(both, width)
    picked = k.a2[:, origin, :, rows_at].reshape(both, UP_ROWS)
    grad = k.e[:, origin].reshape(both, width)
    up_at = pl.ds(pl.multiple_of(piece * UP_ROWS, UP_ROWS), UP_ROWS)
    for c in range(0, width, 256):
        at = pl.ds(pl.multiple_of(piece * width + c, 256), 256)
        bias = k.vec[:, pl.ds(pl.multiple_of(8 * width + piece * width + c, 256), 256)]
        value, slope = gelu_pair(nn(normed, k.wup[:, at]) + bias)
        grad_up = (nt(grad, k.wdown[at, :]) * slope).astype(BF16)
        k.pool[up_at, c : c + 256] += tn(picked, grad_up)
        if down_at is not None:
            k.pool[down_at + c : down_at + c + 256, :] += tn(value.astype(BF16), grad)


def pipeline_kernel(scratch_names, fused, *refs):
    k = Refs(INPUTS + RESULTS + scratch_names, refs)
    sec = lax.axis_index("section")
    count = lax.axis_size("section")
    peers = lax.axis_size("dp")
    me = lax.axis_index("dp")
    micro, rows, width = k.x.shape
    hidden = k.wup.shape[1]
    chips = k.e.shape[1]
    z, core = (me // 2, me % 2) if fused else (0, 0)
    gvec = k.gvec if fused else k.vector_grad
    share = width // peers
    is_first = sec == 0
    is_last = sec == count - 1
    not_last = sec < count - 1
    after = jnp.minimum(sec + 1, count - 1)
    before = jnp.maximum(sec - 1, 0)

    barrier = pltpu.get_barrier_semaphore()

    @pl.when(sec > 0)
    def _():
        pl.semaphore_signal(barrier, inc=1, device_id={"section": before}, device_id_type=MESH)

    @pl.when(not_last)
    def _():
        pl.semaphore_signal(barrier, inc=1, device_id={"section": after}, device_id_type=MESH)

    if fused:
        for step in range(1, peers):
            pl.semaphore_signal(
                barrier, inc=1, device_id={"dp": (me + step) % peers}, device_id_type=MESH
            )

    def patch_copy(m):
        return pltpu.make_async_copy(k.patches.at[m], k.x.at[m], k.psem.at[m])

    def cot_copy(m):
        return pltpu.make_async_copy(k.cot.at[m], k.e.at[m, z], k.csem.at[m])

    loads = [
        pltpu.make_async_copy(src.at[0], dst, k.wsem.at[i])
        for i, (src, dst) in enumerate(
            ((k.wqkv_h, k.wqkv), (k.wout_h, k.wout), (k.wup_h, k.wup), (k.wdown_h, k.wdown))
        )
    ]

    @pl.when(is_first)
    def _():
        for m in range(micro):
            patch_copy(m).start()

    lens_copy = pltpu.make_async_copy(k.lengths, k.lens, k.lsem.at[0])
    lens_copy.start()
    loads[0].start()
    loads[1].start()

    @pl.when(is_last)
    def _():
        for m in range(micro):
            cot_copy(m).start()

    k.bias[:, :width] = k.vec[:, 2 * width : 3 * width]
    k.bias[:, width : 2 * width] = jnp.zeros((1, width), F32)
    k.bias[:, 2 * width :] = k.vec[:, 3 * width : 4 * width]
    gvec[...] = jnp.zeros_like(gvec)
    lens_copy.wait()
    loads[0].wait()
    loads[1].wait()
    loads[2].start()
    loads[3].start()

    def y_send(m):
        return pltpu.make_async_remote_copy(
            src_ref=k.y.at[m], dst_ref=k.x.at[m], send_sem=k.xsend.at[m], recv_sem=k.xrecv.at[m],
            device_id={"section": after}, device_id_type=MESH,
        )

    def e_send(m):
        return pltpu.make_async_remote_copy(
            src_ref=k.y.at[m], dst_ref=k.e.at[m, z], send_sem=k.esend.at[m], recv_sem=k.erecv.at[m],
            device_id={"section": before}, device_id_type=MESH,
        )

    def out_copy(m):
        return pltpu.make_async_copy(k.y.at[m], k.outputs.at[m], k.osem.at[m])

    def in_copy(m):
        return pltpu.make_async_copy(k.ig.at[m], k.input_grads.at[m], k.isem.at[m])

    def to_peer(src, dst, send, recv, device):
        return pltpu.make_async_remote_copy(
            src_ref=src, dst_ref=dst, send_sem=send, recv_sem=recv,
            device_id={"dp": device}, device_id_type=MESH,
        )

    def pass_on(ref, sends, recvs, m, origin, up):
        return to_peer(
            ref.at[m, origin], ref.at[m, origin], sends.at[0 if up else 1, m, origin],
            recvs.at[m, origin], me + 2 if up else me - 2,
        )

    def share_own(ref, sends, recvs, m):
        @pl.when(z < chips - 1)
        def _():
            pass_on(ref, sends, recvs, m, z, True).start()

        @pl.when(z > 0)
        def _():
            pass_on(ref, sends, recvs, m, z, False).start()

    def relay(ref, sends, recvs, m, distance):
        @pl.when(z >= distance)
        def _():
            pass_on(ref, sends, recvs, m, z - distance, True).wait_recv()

            @pl.when(z < chips - 1)
            def _():
                pass_on(ref, sends, recvs, m, z - distance, True).start()

        @pl.when(z + distance < chips)
        def _():
            pass_on(ref, sends, recvs, m, z + distance, False).wait_recv()

            @pl.when(z > 0)
            def _():
                pass_on(ref, sends, recvs, m, z + distance, False).start()

    def settle(ref, sends, recvs, m):
        for distance in range(chips):
            @pl.when((z >= distance) & (z < chips - 1))
            def _():
                pass_on(ref, sends, recvs, m, z - distance, True).wait_send()

            @pl.when((z + distance < chips) & (z > 0))
            def _():
                pass_on(ref, sends, recvs, m, z + distance, False).wait_send()

    if fused:
        acts = (k.a2, k.asend, k.arecv)
        errs = (k.e, k.bsend, k.brecv)
    arrivals = (sec > 0).astype(jnp.int32) + not_last.astype(jnp.int32)
    pl.semaphore_wait(barrier, arrivals + (peers - 1 if fused else 0))

    @pl.when(is_last)
    def _():
        for m in range(micro):
            cot_copy(m).wait()
            valid = lax.broadcasted_iota(jnp.int32, (rows, width), 0) < k.lens[m]
            k.e[m, z] = jnp.where(valid, k.e[m, z].astype(F32), 0.0).astype(BF16)
            if fused:
                share_own(*errs, m)
        if fused:
            for distance in range(1, chips - 1):
                for m in range(micro):
                    relay(*errs, m, distance)

    sibling = me + 1 - 2 * core

    def part_rows(chip, parity):
        return pl.ds(pl.multiple_of(share * (2 * chip + parity), share), share)

    def part_ref(part, chip, parity):
        if part < 3:
            return k.wqkv.at[part_rows(chip, parity), pl.ds(part * width, width)]
        return k.wout.at[part_rows(chip, parity), :]

    def pair_copy(part, chip):
        return to_peer(
            part_ref(part, chip, 1 - core), k.prx.at[part, chip],
            k.pxsend.at[part, chip], k.pxrecv.at[part, chip], sibling,
        )

    def send_pair(part):
        for chip in range(chips):
            pair_copy(part, chip).start()

    ends_first = is_first & not_last if fused else False
    waits_turn = is_first & (core == 1) & not_last

    def forward_step(m):
        @pl.when(is_first)
        def _():
            patch_copy(m).wait()

        @pl.when(sec > 0)
        def _():
            y_send(m).wait_recv()

        key_bias = jnp.where(
            lax.broadcasted_iota(jnp.int32, (1, rows), 1) < k.lens[m], 0.0, -1e30
        )
        forward_attention(k, m, z, key_bias)
        if fused:
            share_own(*acts, m)

            @pl.when(waits_turn & (m > 0))
            def _():
                y_send(m - 1).start()

        @pl.when(m == 0)
        def _():
            loads[2].wait()
            loads[3].wait()

        forward_mlp(k, m, z)

        @pl.when(not_last & jnp.logical_not(waits_turn))
        def _():
            y_send(m).start()

        out_copy(m).start()

    def relay_acts(*distances):
        for distance in distances:
            for m in range(micro):
                relay(*acts, m, distance)

    def backward_step(m):
        out_copy(m).wait()

        @pl.when(not_last)
        def _():
            e_send(m).wait_recv()
            if fused:
                share_own(*errs, m)

        backward_mlp(k, gvec, m, z)
        backward_out(k, m)
        if fused:
            @pl.when(ends_first & (m == micro - 1))
            def _():
                out_weight_grad(k)
                send_pair(3)
                for early in range(micro - 1):
                    relay(*errs, early, 2)

        backward_heads(k, gvec, m)

        backward_qkv(k, gvec, m)

        @pl.when(sec > 0)
        def _():
            e_send(m).start()

        in_copy(m).start()
        if fused:
            @pl.when(ends_first & (m < micro - 1))
            def _():
                relay(*errs, m, 1)

    def turn_round():
        if fused:
            @pl.when(is_first & (core == 0) & not_last)
            def _():
                y_send(micro - 1).wait_send()
                pl.semaphore_signal(k.turn, inc=1, device_id={"dp": me + 1}, device_id_type=MESH)

            @pl.when(waits_turn)
            def _():
                pl.semaphore_wait(k.turn, 1)
                y_send(micro - 1).start()
        for m in range(micro):
            waited = is_first & (core == 0) if fused and m == micro - 1 else False

            @pl.when(jnp.logical_not(waited))
            def _():
                y_send(m).wait_send()

        if fused:
            relay_acts(1)
            pl.when(sec < count - 2)(lambda: relay_acts(*range(2, chips - 1)))

    def step(index, carry):
        forward = jnp.where(is_last, index % 2 == 0, index < micro)
        m = jnp.where(is_last, index // 2, index % micro)
        pl.when(forward)(lambda: forward_step(m))
        pl.when(not_last & (index == micro))(turn_round)
        pl.when(jnp.logical_not(forward))(lambda: backward_step(m))
        return carry

    lax.fori_loop(0, 2 * micro, step, 0)

    def finish_hops():
        for m in range(micro):
            in_copy(m).wait()

            @pl.when(sec > 0)
            def _():
                e_send(m).wait_send()

    if not fused:
        out_weight_grad(k)
        qkv_weight_grads(k, lambda part: None)
        for c in range(0, hidden, width):
            mlp_weight_grads(k, 0, c, True)
            k.wup[:, c : c + width] = k.pool[:width, :].astype(BF16)
            k.wdown[c : c + width, :] = k.pool[width:, :].astype(BF16)
        copies = [
            pltpu.make_async_copy(src, dst, k.wsem.at[i])
            for i, (src, dst) in enumerate(
                ((k.wqkv, k.qkv_grad), (k.wout, k.out_grad), (k.wup, k.up_grad), (k.wdown, k.down_grad))
            )
        ]
        for copy in copies:
            copy.start()
        for copy in copies:
            copy.wait()
        finish_hops()
        return

    @pl.when(jnp.logical_not(ends_first))
    def _():
        out_weight_grad(k)
        send_pair(3)

    qkv_weight_grads(k, send_pair)

    length = gvec.shape[1] // peers

    def vector_copy(step):
        device = (me + step) % peers
        return to_peer(
            gvec.at[:, pl.ds(pl.multiple_of(device * length, 128), length)], k.vrx.at[step],
            k.vsend.at[step], k.vrecv.at[step], device,
        )

    for step in range(1, peers):
        vector_copy(step).start()

    def chain_copy(up, part, place):
        chip = place if up else chips - 1 - place
        lane = 0 if up else 1
        return to_peer(
            part_ref(part, chip, core), k.rsx.at[lane, part, place - 1],
            k.rsend.at[lane, part, place], k.rrecv.at[lane, part, place],
            me + 2 if up else me - 2,
        )

    def chain(stage, place, parts=range(4)):
        for up in (True, False):
            @pl.when((z if up else chips - 1 - z) == stage)
            def _():
                chip = place if up else chips - 1 - place
                for part in parts:
                    if stage > 0:
                        chain_copy(up, part, place).wait_recv()
                        target = part_ref(part, chip, core)
                        target[...] = (
                            target[...].astype(F32)
                            + k.rsx[0 if up else 1, part, place - 1].astype(F32)
                        ).astype(BF16)
                    chain_copy(up, part, place).start()

    for part in (3, 0, 1, 2):
        for chip in range(chips):
            pair_copy(part, chip).wait()
            target = part_ref(part, chip, core)
            target[...] = (target[...].astype(F32) + k.prx[part, chip].astype(F32)).astype(BF16)
        chain(0, chips - 1, (part,))

    def follow(place):
        for up in (True, False):
            @pl.when((z if up else chips - 1 - z) == 0)
            def _():
                for part in range(4):
                    chain_copy(up, part, place + 1).wait_send()
                for part in range(4):
                    chain_copy(up, part, place).start()

    @pl.when(not_last & (sec > 0))
    def _():
        for early in range(micro - 1):
            relay(*errs, early, 1)

    @pl.when(not_last)
    def _():
        relay(*errs, micro - 1, 1)

    @pl.when(not_last & (sec > 0))
    def _():
        for early in range(micro - 1):
            relay(*errs, early, 2)

    pl.when(is_last)(lambda: relay_acts(1))
    pl.when(sec >= count - 2)(lambda: relay_acts(*range(2, chips - 1)))
    def nearby(index):
        low = z + (index % 2) * (1 - 2 * (z % 2))
        return low + (index // 2) * (2 - 4 * ((low // 2) % 2))

    rows_at = pl.ds(pl.multiple_of(128 * ((3 * z) // 2), 128), UP_ROWS)
    down_base = chips * UP_ROWS

    def batch(origin, hooks=()):
        slice_weight_grads(k, origin, z, rows_at, down_base)

        def other(step, carry):
            for at, hook in hooks:
                pl.when(step == at)(hook)
            slice_weight_grads(k, origin, (z + step) % chips, rows_at, None)
            return carry

        lax.fori_loop(1, chips, other, 0)

    inner = (z > 0) & (z < chips - 1)

    def relay_inner():
        @pl.when(not_last & inner)
        def _():
            relay(*errs, micro - 1, 2)

    outward = (3, 0, 1, 2)
    own_weight_grads(k, z, rows_at, down_base)
    batch(nearby(1), ((2, relay_inner), (2, lambda: follow(2))))
    chain(1, 3, outward)

    @pl.when(not_last & jnp.logical_not(inner))
    def _():
        relay(*errs, micro - 1, 2)

    batch(nearby(2))
    follow(1)
    chain(1, 2)
    for m in range(micro):
        relay(*acts, m, chips - 1)
        relay(*errs, m, chips - 1)
    chain(2, 3, outward)
    batch(nearby(3))

    per_core = hidden // peers

    def down_rows(parity):
        return pl.ds(pl.multiple_of(down_base + per_core * parity, 128), per_core)

    def up_rows(piece, parity):
        first_row = UP_ROWS * piece + (UP_ROWS - 2 * share) * (z % 2) + share * parity
        return pl.ds(pl.multiple_of(first_row, 32), share)

    for piece in range(chips):
        k.upx[piece] = k.pool[up_rows(piece, 1 - core), :].astype(BF16)
    up_pair = to_peer(k.upx, k.uprx, k.upsem.at[0], k.upsem.at[1], sibling)
    up_pair.start()
    k.dnx[...] = k.pool[down_rows(1 - core), :].astype(BF16)
    down_pair = to_peer(k.dnx, k.dnrx, k.dnsem.at[0], k.dnsem.at[1], sibling)
    down_pair.start()
    finals = []
    up_pair.wait()
    for piece in range(chips):
        at = up_rows(piece, core)
        k.pool[at, :] += k.uprx[piece].astype(F32)
        final = pltpu.make_async_copy(
            k.pool.at[at], k.up_grad.at[:, pl.ds(piece * width, width)], k.gsem.at[5 + piece]
        )
        final.start()
        finals.append(final)
    down_pair.wait()
    k.pool[down_rows(core), :] += k.dnrx[...].astype(F32)
    final = pltpu.make_async_copy(k.pool.at[down_rows(core)], k.down_grad, k.gsem.at[0])
    final.start()
    finals.append(final)
    finish_hops()

    for part in range(4):
        held = k.ig.at[part // 2, pl.ds(share * (part % 2), share)]
        held[...] = part_ref(part, z, core)[...].astype(F32)

        @pl.when(z > 0)
        def _():
            chain_copy(True, part, z).wait_recv()
            held[...] += k.rsx[0, part, z - 1].astype(F32)

        @pl.when(z < chips - 1)
        def _():
            chain_copy(False, part, chips - 1 - z).wait_recv()
            held[...] += k.rsx[1, part, chips - 2 - z].astype(F32)

        target = k.qkv_grad.at[:, pl.ds(part * width, width)] if part < 3 else k.out_grad
        final = pltpu.make_async_copy(held, target, k.gsem.at[1 + part])
        final.start()
        finals.append(final)
    own = gvec[:, pl.ds(pl.multiple_of(me * length, 128), length)]
    for step in range(1, peers):
        vector_copy(step).wait()
        own = own + k.vrx[step]
    k.vector_grad[...] = own

    for m in range(micro):
        settle(*acts, m)
        settle(*errs, m)
    for part in range(4):
        for up in (True, False):
            for place in range(1, chips):
                position = z if up else chips - 1 - z

                @pl.when((position < place) & ((position > 0) | (place == 1)))
                def _():
                    chain_copy(up, part, place).wait_send()
    for final in finals:
        final.wait()


def deliver_kernel(count, *refs):
    sources, targets, held = refs[:count], refs[count : 2 * count], refs[2 * count : 3 * count]
    sems = refs[-1]
    fetches = [
        pltpu.make_async_copy(sources[i], held[i], sems.at[0, i]) for i in range(count)
    ]
    stores = [
        pltpu.make_async_copy(held[i], targets[i], sems.at[1, i]) for i in range(count)
    ]
    for fetch in fetches:
        fetch.start()
    for fetch, store in zip(fetches, stores):
        fetch.wait()
        store.start()
    for store in stores:
        store.wait()


def deliver(arrays):
    anywhere = pl.BlockSpec(memory_space=pl.ANY)
    count = len(arrays)
    return pl.pallas_call(
        partial(deliver_kernel, count),
        out_shape=tuple(jax.ShapeDtypeStruct(a.shape, a.dtype) for a in arrays),
        in_specs=[anywhere] * count,
        out_specs=(anywhere,) * count,
        scratch_shapes=[pltpu.VMEM(a.shape, a.dtype) for a in arrays]
        + [pltpu.SemaphoreType.DMA((2, count))],
        compiler_params=pltpu.CompilerParams(vmem_limit_bytes=62 << 20),
    )(*arrays)


def shards(patches, lengths, qkv_weight, out_weight, up_weight, down_weight, vectors, cotangent):
    micro, _, rows, width = patches.shape
    hidden = up_weight.shape[2]
    peers = lax.axis_size("dp")
    fused = peers == 8 and hidden == peers // 2 * width and 4 * (width // peers) == 3 * 128
    chips = peers // 2 if fused else 1
    plan = scratch_plan(micro, rows, width, hidden, chips, peers, fused)
    anywhere = pl.BlockSpec(memory_space=pl.ANY)
    in_vmem = pl.BlockSpec(memory_space=pltpu.VMEM)
    kept = F32 if fused else BF16
    cut = peers if fused else 1
    results = pl.pallas_call(
        partial(pipeline_kernel, tuple(plan), fused),
        out_shape=(
            jax.ShapeDtypeStruct((micro, rows, width), BF16),
            jax.ShapeDtypeStruct((micro, rows, width), F32),
            jax.ShapeDtypeStruct((width // cut, 3 * width), kept),
            jax.ShapeDtypeStruct((width // cut, width), kept),
            jax.ShapeDtypeStruct((width // cut, hidden), kept),
            jax.ShapeDtypeStruct((hidden // cut, width), kept),
            jax.ShapeDtypeStruct((1, vectors.shape[1] // cut), F32),
        ),
        in_specs=[
            anywhere,
            anywhere,
            anywhere,
            anywhere,
            anywhere,
            anywhere,
            in_vmem,
            anywhere,
        ],
        out_specs=(anywhere,) * 6 + (in_vmem,),
        scratch_shapes=list(plan.values()),
        compiler_params=pltpu.CompilerParams(
            collective_id=0, has_side_effects=True, vmem_limit_bytes=62 << 20
        ),
    )(
        patches[:, 0],
        lengths[:, 0],
        qkv_weight,
        out_weight,
        up_weight,
        down_weight,
        vectors,
        cotangent[:, 0],
    )
    if fused:
        results = deliver(results)
    outputs, input_grads, *grads, vector_grad = results
    if fused:
        grads = [grad[None] for grad in grads]
    else:
        grads = [
            lax.psum_scatter(grad[None], "dp", scatter_dimension=1, tiled=True).astype(F32)
            for grad in grads
        ]
        vector_grad = lax.psum_scatter(vector_grad, "dp", scatter_dimension=1, tiled=True)
    return (outputs[None, :, None], input_grads[None, :, None], *grads, vector_grad)


def solution(mesh):
    placed = (
        P(None, "dp", None, None),
        P(None, "dp"),
        P("section", None, None),
        P("section", None, None),
        P("section", None, None),
        P("section", None, None),
        P("section", None),
        P(None, "dp", None, None),
    )
    return jax.shard_map(
        shards,
        mesh=mesh,
        in_specs=placed,
        out_specs=(
            P("section", None, "dp", None, None),
            P("section", None, "dp", None, None),
            P("section", "dp", None),
            P("section", "dp", None),
            P("section", "dp", None),
            P("section", "dp", None),
            P("section", "dp"),
        ),
        check_vma=False,
    )
```
